256 devices in a mesh: pipe: 8 (over x, y_hi), ctx: 32 (over y_lo, z, core).
Axes of the slice: x: 4, y: 4 (y_hi: 2, y_lo: 2; y = y_hi * 2 + y_lo), z: 8, core: 2. Of those that a mesh axis runs over, the one named last changes fastest.
Arguments:
- queries: bfloat16 [8, 4096, 4096], P('pipe', 'ctx'), may hold values from -6 to 6
- outputs_fwd: bfloat16 [8, 4096, 4096], P('pipe', 'ctx'), may hold values from -3 to 3
- handed_grads: bfloat16 [8, 4096, 4096], P('pipe', 'ctx'), may hold values from -1.5 to 1.5
- log_norms: float32 [8, 4096, 32], P('pipe', 'ctx'), may hold values from 2 to 4
- own_keys: bfloat16 [8, 4096, 512], P('pipe', 'ctx'), may hold values from -6 to 6
- own_values: bfloat16 [8, 4096, 512], P('pipe', 'ctx'), may hold values from -6 to 6
- pool_keys: bfloat16 [8, 2048, 512], P('pipe', 'ctx'), may hold values from -6 to 6
- pool_values: bfloat16 [8, 2048, 512], P('pipe', 'ctx'), may hold values from -6 to 6
- block_tables: int32 [8, 64, 32], P('pipe', 'ctx'), may hold values from -1 to 63, as said below
- lengths: int32 [8, 64], P('pipe', 'ctx'), may hold values from 1 to 64, 3072 in all within a row
Outputs:
- grad_queries: bfloat16 [8, 4096, 4096], P('pipe', 'ctx')
- grad_own_keys: bfloat16 [8, 4096, 512], P('pipe', 'ctx')
- grad_own_values: bfloat16 [8, 4096, 512], P('pipe', 'ctx')
- grad_pool_keys: float32 [8, 2048, 512], P('pipe', 'ctx')
- grad_pool_values: float32 [8, 2048, 512], P('pipe', 'ctx')
The draws below stay inside these ranges and needn't reach their ends.
Inputs may be any that keep to these rules, and one draw needn't show every extreme that they name: `block_tables`: each response lists prompt block numbers in its first 1 to 32 entries (repeats allowed) and -1 in the rest; in every section some response uses all 32 entries. `lengths`: in every section the longest response has exactly 64 tokens.
All inputs are finite; a program needn't handle non-finite values. No bound on the sum of `lengths` on one device may be relied on, other than what follows from the above.
Results may differ from the reference program's by a relative error of at most 0.0063.
Values may be sent and summed in bfloat16 or wider, within the bound.
A program may use at most 128 MiB of HBM per device.

```python
import math
from functools import partial
import jax
import jax.numpy as jnp
import numpy as np
from jax import lax

HQ = 32
KVH = 4
HD = 128
BLK = 32
RLEN = 64
SECTIONS = 8
NRESP = 64
QROWS = 4096
NBLK = 64
POOL = 2048
TBL = 32


def draw_block_tables(key, part):
    key = jax.random.fold_in(key, 11)
    shared_key, spread_key, choose_key, count_key = jax.random.split(key, 4)
    table_shape = (SECTIONS, NRESP, TBL)
    shared = jax.random.randint(shared_key, (SECTIONS, 1, TBL), 0, NBLK)
    spread = jax.random.randint(spread_key, table_shape, 0, NBLK)
    choose = jax.random.randint(choose_key, table_shape, 0, 2)
    block_ids = jnp.where(choose == 1, shared, spread)
    block_ids = block_ids.at[:, 0, 0].set(NBLK - 1)
    counts = jax.random.randint(count_key, (SECTIONS, NRESP, 1), 1, TBL + 1)
    counts = counts.at[:, 0, :].set(TBL)
    position = jnp.arange(TBL, dtype=jnp.int32)[None, None, :]
    return jnp.where(position < counts, block_ids, -1).astype(jnp.int32)


def shard_levels(own_key, extent, pieces, low, high):
    factor_of = 1.0
    for dim, blocks in pieces:
        heights = jax.random.uniform(jax.random.fold_in(jax.random.fold_in(own_key, 6), dim), (blocks,), jnp.float32, low / len(pieces), high / len(pieces))
        factor_of = factor_of * jnp.repeat(jnp.exp(heights), extent[dim] // blocks).reshape((-1,) + (1,) * (len(extent) - 1 - dim))
    return factor_of


def profile(count, total, limit, skew):
    weights = [(1 << 20) // math.isqrt(grade ** skew) + 1 for grade in range(2, count + 1)]
    surplus, given = total - limit - (count - 1), [1] * (count - 1)
    while surplus > 0:
        free = [i for i in range(count - 1) if given[i] < limit]
        mass, remaining = sum([weights[i] for i in free]), surplus
        for i in free:
            addition = min(limit - given[i], max(1, remaining * weights[i] // mass), surplus)
            given[i] = given[i] + addition
            surplus = surplus - addition
    return np.array([limit] + given)


def uneven_parts(stream_key, amount, total, bound, lean):
    if amount == 2:
        one = jax.random.randint(stream_key, (), max(1, total - bound), min(bound, total - 1) + 1)
        return jnp.stack([one, total - one])
    sizes = jnp.asarray(profile(amount, total, bound, lean), jnp.int32)
    twos = (amount - 1) // 2
    donor, receiver = sizes[1:1 + 2 * twos:2], sizes[2:2 + 2 * twos:2]
    margin = jnp.minimum(donor - 1, bound - receiver)
    passed = jax.random.randint(jax.random.fold_in(stream_key, 1), (twos,), 0, 1 << 20) % (margin + 1)
    sizes = sizes.at[1:1 + 2 * twos:2].set(donor - passed).at[2:2 + 2 * twos:2].set(receiver + passed)
    return sizes[jax.random.permutation(jax.random.fold_in(stream_key, 2), amount)]


def scatter_about(rng, shape, deviation, bound, shards=(), kind=jnp.bfloat16):
    values = jax.random.normal(rng, shape, jnp.float32) * deviation
    if len(shards) > 0:
        values = shard_levels(rng, shape, shards, -0.22, 0.18) * values
    return jnp.clip(values, min=-bound, max=bound).astype(kind)


def setup_inputs(seed: int = 0) -> dict:
    splits = jax.random.split(jax.random.key(seed), 11)
    return {
        "queries": scatter_about(splits[0], (SECTIONS, QROWS, HQ * HD), 1.0, 6.0, ((0, 8), (1, 32))),
        "outputs_fwd": scatter_about(splits[1], (SECTIONS, QROWS, HQ * HD), 0.5, 3.0, ((0, 8), (1, 32))),
        "handed_grads": scatter_about(splits[2], (SECTIONS, QROWS, HQ * HD), 0.25, 1.5, ((0, 8), (1, 32))),
        "log_norms": jnp.clip(2.0 + 2.0 * jax.random.uniform(splits[3], (SECTIONS, QROWS, HQ), jnp.float32) ** shard_levels(splits[3], (SECTIONS, QROWS, HQ), ((0, 8), (1, 32)), -0.2, 0.2), 2.0, 4.0),
        "own_keys": scatter_about(splits[4], (SECTIONS, QROWS, KVH * HD), 1.0, 6.0, ((0, 8), (1, 32))),
        "own_values": scatter_about(splits[5], (SECTIONS, QROWS, KVH * HD), 1.0, 6.0, ((0, 8), (1, 32))),
        "pool_keys": scatter_about(splits[6], (SECTIONS, POOL, KVH * HD), 1.0, 6.0, ((0, 8), (1, 32))),
        "pool_values": scatter_about(splits[7], (SECTIONS, POOL, KVH * HD), 1.0, 6.0, ((0, 8), (1, 32))),
        "block_tables": draw_block_tables(jax.random.fold_in(splits[10], 71), 0),
        "lengths": jax.vmap(lambda own: uneven_parts(own, NRESP, NRESP * RLEN * 3 // 4, RLEN, 1))(jax.random.split(splits[9], SECTIONS)).reshape((SECTIONS, NRESP)).astype(jnp.int32),
    }


def split_heads(matrix):
    row_count = matrix.shape[0]
    return matrix.reshape(row_count, KVH, HQ // KVH, HD).transpose(1, 2, 0, 3)


def merge_heads(grad_heads):
    row_count = grad_heads.shape[2]
    return grad_heads.transpose(2, 0, 1, 3).reshape(row_count, HQ * HD)


def head_inputs(queries, fwd_out, cotangent, log_norms):
    row_count = queries.shape[0]
    products = cotangent.astype(jnp.float32) * fwd_out.astype(jnp.float32)
    row_dots = jnp.sum(products.reshape(row_count, HQ, HD), axis=-1)
    norm_heads = log_norms.reshape(row_count, KVH, HQ // KVH).transpose(1, 2, 0)
    dot_heads = row_dots.reshape(row_count, KVH, HQ // KVH).transpose(1, 2, 0)
    return (split_heads(queries.astype(jnp.float32)), split_heads(cotangent.astype(jnp.float32)), norm_heads, dot_heads)


def key_terms(head_data, key_rows, value_rows, visible):
    query_heads, grad_heads, norm_heads, dot_heads = head_data
    score_scale = HD ** -0.5
    key_count = key_rows.shape[0]
    key_heads = key_rows.astype(jnp.float32).reshape(key_count, KVH, HD).transpose(1, 0, 2)
    value_heads = value_rows.astype(jnp.float32).reshape(key_count, KVH, HD).transpose(1, 0, 2)
    scores = jnp.einsum("hgrd,hnd->hgrn", query_heads, key_heads) * score_scale
    probs = jnp.where(visible[None, None], jnp.exp(scores - norm_heads[..., None]), 0.0)
    probs_low = lax.optimization_barrier(probs.astype(jnp.bfloat16)).astype(jnp.float32)
    dprobs = jnp.einsum("hgrd,hnd->hgrn", grad_heads, value_heads)
    dscores = probs * (dprobs - dot_heads[..., None])
    dscores_low = lax.optimization_barrier(dscores.astype(jnp.bfloat16)).astype(jnp.float32)
    grad_query = jnp.einsum("hgrn,hnd->hgrd", dscores_low, key_heads) * score_scale
    grad_key = jnp.einsum("hgrn,hgrd->hnd", dscores_low, query_heads) * score_scale
    grad_value = jnp.einsum("hgrn,hgrd->hnd", probs_low, grad_heads)
    grad_key = grad_key.transpose(1, 0, 2).reshape(key_count, KVH * HD)
    grad_value = grad_value.transpose(1, 0, 2).reshape(key_count, KVH * HD)
    return grad_query, grad_key, grad_value


def response_terms(pool_keys, pool_values, running, inputs):
    queries, fwd_out, cotangent, log_norms, own_keys, own_values, table_row, resp_length = inputs
    head_data = head_inputs(queries, fwd_out, cotangent, log_norms)
    position = jnp.arange(RLEN, dtype=jnp.int32)
    live_rows = position < resp_length
    block_ids = jnp.arange(POOL, dtype=jnp.int32) // BLK
    listed = jnp.any(table_row[:, None] == block_ids[None, :], axis=0)
    pool_visible = live_rows[:, None] & listed[None, :]
    own_visible = live_rows[:, None] & (position[None, :] <= position[:, None])
    pool_q, pool_k, pool_v = key_terms(head_data, pool_keys, pool_values, pool_visible)
    own_q, own_k, own_v = key_terms(head_data, own_keys, own_values, own_visible)
    grad_query = merge_heads(pool_q + own_q).astype(jnp.bfloat16)
    running = running + jnp.concatenate([pool_k, pool_v], axis=1)
    return running, (grad_query, own_k.astype(jnp.bfloat16), own_v.astype(jnp.bfloat16))


def per_response(matrix):
    return matrix.reshape(NRESP, RLEN, matrix.shape[-1])


def section_terms(inputs):
    queries, fwd_out, cotangent, log_norms, own_keys, own_values, pool_keys, pool_values, tables, resp_lengths = inputs
    running = jnp.zeros((POOL, 2 * KVH * HD), jnp.float32)
    scanned = (per_response(queries), per_response(fwd_out), per_response(cotangent), per_response(log_norms),
               per_response(own_keys), per_response(own_values), tables, resp_lengths)
    running, outputs = lax.scan(partial(response_terms, pool_keys, pool_values), running, scanned)
    grad_query, grad_own_k, grad_own_v = outputs
    return (grad_query.reshape(QROWS, HQ * HD), grad_own_k.reshape(QROWS, KVH * HD),
            grad_own_v.reshape(QROWS, KVH * HD), running[:, :KVH * HD], running[:, KVH * HD:])


def reference(queries, outputs_fwd, handed_grads, log_norms, own_keys, own_values, pool_keys, pool_values, block_tables, lengths):
    cotangent = jnp.roll(handed_grads, -1, axis=0)
    grad_queries, grad_own_keys, grad_own_values, grad_pool_keys, grad_pool_values = lax.map(
        section_terms, (queries, outputs_fwd, cotangent, log_norms, own_keys, own_values, pool_keys, pool_values, block_tables, lengths))
    return (grad_queries, grad_own_keys, grad_own_values, grad_pool_keys, grad_pool_values)
```

```python
import functools
import math

import jax
import jax.numpy as jnp
from jax import lax
from jax.experimental import pallas as pl
from jax.experimental.pallas import tpu as pltpu
from jax.sharding import PartitionSpec as P

HD = 128
ROWS = 128
RLEN = 64
BLK = 32
GROUP = 8
SCALE = HD ** -0.5
EXP_SCALE = SCALE * math.log2(math.e)
FAR = 1e30
BF = jnp.bfloat16
F32 = jnp.float32
MESH = pl.DeviceIdType.MESH


def split3(x):
    hi = x.astype(BF).astype(F32)
    rest = x - hi
    mid = rest.astype(BF).astype(F32)
    return hi, mid, rest - mid


def dot(a, b):
    return jnp.dot(a, b, preferred_element_type=F32)


def kernel(
    zs, pipes,
    q_hbm, o_hbm, g_hbm, ln_ref, ok_hbm, ov_hbm, pk_hbm, pv_hbm, tab_ref, len_ref,
    dq_out, dok_out, dov_out, dpk_out, dpv_out,
    qb, ob, cb, qh, ch, qt, ct, kv, kaug, okv, dqt, ds_s, p_s,
    send_buf, recv_buf, fin, fsend, frecv, dq_st, ok_st, ln_t, ln_r, bp_s, bp,
    loc_sem, sib_send, sib_recv, cot_send, cot_recv, kv_send, kv_recv,
    ga_send, ga_recv, rs_send, rs_recv, f_send, f_recv, out_sem, out_send, out_recv,
):
    p = lax.axis_index("pipe")
    c = lax.axis_index("ctx")
    core = lax.rem(c, 2)
    z = lax.rem(lax.div(c, 2), zs)
    yl = lax.div(c, 2 * zs)
    oc = 1 - core

    def dev(pp, yy, zz, kk):
        return (pp, (yy * zs + zz) * 2 + kk)

    sib = dev(p, yl, z, oc)
    z_up = lax.rem(z + 1, zs)
    z_dn = lax.rem(z + zs - 1, zs)
    p_up = lax.rem(p + 1, pipes)
    p_dn = lax.rem(p + pipes - 1, pipes)
    ring_dst = (dev(p, yl, z_up, core), dev(p, yl, z_dn, core))

    def half(ref, kk, width):
        return ref.at[:, pl.ds(pl.multiple_of(kk * width, 128), width)]

    def remote(src, dst, ss, rs, to):
        return pltpu.make_async_remote_copy(
            src_ref=src, dst_ref=dst, send_sem=ss, recv_sem=rs, device_id=to, device_id_type=MESH
        )

    my_rows = pl.ds(pl.multiple_of(core * ROWS, ROWS), ROWS)
    my_half = pl.ds(pl.multiple_of(core * 64, 64), 64)
    my_chunk = yl * zs + z

    loc = [
        pltpu.make_async_copy(half(q_hbm, core, 2048), qb.at[my_rows], loc_sem.at[0]),
        pltpu.make_async_copy(half(o_hbm, core, 2048), ob.at[my_rows], loc_sem.at[1]),
        pltpu.make_async_copy(half(ok_hbm, core, 256), okv.at[my_rows, 0:256], loc_sem.at[2]),
        pltpu.make_async_copy(half(ov_hbm, core, 256), okv.at[my_rows, 256:512], loc_sem.at[3]),
        pltpu.make_async_copy(half(pk_hbm, core, 256), kv.at[my_chunk, my_half, 0:256], loc_sem.at[4]),
        pltpu.make_async_copy(half(pv_hbm, core, 256), kv.at[my_chunk, my_half, 256:512], loc_sem.at[5]),
    ]
    for cp in loc:
        cp.start()

    row = lax.broadcasted_iota(jnp.int32, (ROWS, 32), 0)
    length = jnp.where(row < RLEN, len_ref[0, 0], len_ref[0, 1])
    live = lax.rem(row, RLEN) < length
    ln_t[...] = jnp.where(live, ln_ref[...] * (1.0 / SCALE), FAR).T
    lane = lax.broadcasted_iota(jnp.int32, bp_s.shape, 1)
    ids = lax.broadcasted_iota(jnp.int32, (bp_s.shape[0], tab_ref.shape[1]), 0)
    offs = jnp.zeros(bp_s.shape, F32)
    for rr in range(2):
        hit = jnp.where(tab_ref[rr : rr + 1, :] == ids, 1.0, 0.0)
        listed = jnp.max(hit, axis=1, keepdims=True)
        offs = jnp.where(lane == 3 + 2 * core + rr, (listed - 1.0) * FAR, offs)
    bp_s[...] = offs
    bp[core] = offs
    ln_r[core] = ln_t[pl.ds(pl.multiple_of(core * 16, 16), 16), :]

    barrier = pltpu.get_barrier_semaphore()
    partners = [
        sib,
        dev(p, 1 - yl, z, 0), dev(p, 1 - yl, z, 1),
        ring_dst[0], ring_dst[1],
        dev(p_dn, yl, z, 0), dev(p_dn, yl, z, 1),
        dev(p_up, yl, z, 0), dev(p_up, yl, z, 1),
    ]
    for to in partners:
        pl.semaphore_signal(barrier, inc=1, device_id=to, device_id_type=MESH)
    pl.semaphore_wait(barrier, len(partners))

    group = [(yl, oc), (1 - yl, core), (1 - yl, oc)]
    kv_out = []
    for i, (yy, kk) in enumerate(group):
        for j, src in enumerate((pk_hbm, pv_hbm)):
            kv_out.append(
                remote(
                    half(src, kk, 256),
                    kv.at[my_chunk, my_half, j * 256 : (j + 1) * 256],
                    kv_send.at[i, j], kv_recv.at[i, j], dev(p, yy, z, kk),
                )
            )
    for cp in kv_out:
        cp.start()

    cot_out = []
    for j in range(2):
        for d in range(2):
            kk = jnp.where(d == 0, oc, core)
            cot_out.append(
                remote(
                    g_hbm.at[:, pl.ds(pl.multiple_of(kk * 2048 + j * 1024, 128), 1024)],
                    cb.at[my_rows, j * 1024 : (j + 1) * 1024],
                    cot_send.at[j, d], cot_recv.at[j, d], dev(p_dn, yl, z, kk),
                )
            )
    for cp in cot_out:
        cp.start()

    sib_out = [
        remote(half(q_hbm, oc, 2048), qb.at[my_rows], sib_send.at[0], sib_recv.at[0], sib),
        remote(half(o_hbm, oc, 2048), ob.at[my_rows], sib_send.at[1], sib_recv.at[1], sib),
        remote(half(ok_hbm, oc, 256), okv.at[my_rows, 0:256], sib_send.at[2], sib_recv.at[2], sib),
        remote(half(ov_hbm, oc, 256), okv.at[my_rows, 256:512], sib_send.at[3], sib_recv.at[3], sib),
        remote(ln_t.at[pl.ds(pl.multiple_of(oc * 16, 16), 16)], ln_r.at[core], sib_send.at[4], sib_recv.at[4], sib),
        remote(bp_s, bp.at[core], sib_send.at[5], sib_recv.at[5], sib),
    ]
    for cp in sib_out:
        cp.start()

    def chunk_id(d, t):
        return lax.rem(z + zs - t, zs) if d == 0 else zs + lax.rem(z + t, zs)

    def gather(d, t):
        ref = kv.at[chunk_id(d, t)]
        return remote(ref, ref, ga_send.at[d, t], ga_recv.at[d, t], ring_dst[d])

    def gather_wait(d, t):
        ref = kv.at[chunk_id(d, t + 1)]
        remote(ref, ref, ga_send.at[d, t], ga_recv.at[d, t], ring_dst[d]).wait_recv()

    loc[4].wait()
    loc[5].wait()
    for cp in kv_out:
        cp.wait_recv()
    for d in range(2):
        gather(d, 0).start()

    qt[:, 128:256, :] = jnp.zeros((2, 128, 2048), BF)
    ct[:, 128:256, :] = jnp.zeros((2, 128, 2048), BF)
    recv_buf[:, 0] = jnp.zeros(recv_buf.shape[:1] + recv_buf.shape[2:], BF)
    loc[0].wait()
    sib_out[0].wait_recv()
    sib_out[4].wait_recv()
    sub = lax.broadcasted_iota(jnp.int32, (16, 128), 0)
    col = lax.broadcasted_iota(jnp.int32, (16, 128), 1)

    def tile_cols(side, g):
        return slice(side * 1024 + g * 128, side * 1024 + (g + 1) * 128)

    def query_tiles(h, side):
        for g in range(GROUP):
            cols = tile_cols(side, g)
            tile = qb[side * 128 : (side + 1) * 128, (h * 8 + g) * 128 : (h * 8 + g + 1) * 128]
            qh[h, cols, :] = tile
            qt[h, 0:128, cols] = tile.T
            hi, mid, low = split3(ln_r[side, h * 8 + g : h * 8 + g + 1, :])
            own = jnp.where(sub - 3 == side * 2 + lax.div(col, RLEN), 1.0, 0.0)
            aug = jnp.where(sub == 0, -hi, jnp.where(sub == 1, -mid, jnp.where(sub == 2, -low, own)))
            qt[h, 128:144, cols] = aug.astype(BF)

    def cot_tiles(h, side):
        for g in range(GROUP):
            cols = tile_cols(side, g)
            rows, lanes = slice(side * 128, (side + 1) * 128), slice((h * 8 + g) * 128, (h * 8 + g + 1) * 128)
            tile = cb[rows, lanes]
            ch[h, cols, :] = tile
            tile_t = tile.T
            ct[h, 0:128, cols] = tile_t
            prod = tile_t.astype(F32) * ob[rows, lanes].T.astype(F32)
            hi, mid, low = split3(jnp.sum(prod, axis=0, keepdims=True))
            aug = jnp.where(sub == 0, hi, jnp.where(sub == 1, mid, jnp.where(sub == 2, low, 0.0)))
            ct[h, 128:144, cols] = aug.astype(BF)

    for h in range(2):
        for side in range(2):
            query_tiles(h, side)

    def gather_step(t, carry):
        for d in range(2):
            gather_wait(d, t - 1)
            gather(d, t).start()
        return carry

    lax.fori_loop(1, zs - 1, gather_step, 0)

    sib_out[5].wait_recv()
    aug_lane = lax.broadcasted_iota(jnp.int32, bp_s.shape, 1)
    blocks = bp[0] + bp[1] + jnp.where(aug_lane < 3, 1.0, 0.0)
    spread = jnp.broadcast_to(blocks[:, None, :], (blocks.shape[0], BLK, 128))
    kaug[...] = spread.reshape(kaug.shape).astype(BF)

    loc[1].wait()
    sib_out[1].wait_recv()
    for cp in cot_out:
        cp.wait_recv()
    for h in range(2):
        for side in range(2):
            cot_tiles(h, side)

    for i in (2, 3):
        loc[i].wait()
        sib_out[i].wait_recv()
    one_lane = lax.broadcasted_iota(jnp.int32, (256, 128), 1) < 3
    v_cst = jnp.where(one_lane, -1.0, 0.0).astype(BF)
    k_cst = jnp.where(one_lane, 1.0, 0.0).astype(BF)
    key_i = lax.broadcasted_iota(jnp.int32, (ROWS, 1024), 0)
    row_i = lax.rem(lax.broadcasted_iota(jnp.int32, (ROWS, 1024), 1), ROWS)
    seen = (lax.div(key_i, RLEN) == lax.div(row_i, RLEN)) & (key_i <= row_i)
    for h in range(2):
        for side in range(2):
            rows = slice(side * 128, (side + 1) * 128)
            cols = slice(side * 1024, (side + 1) * 1024)
            k_l = okv[rows, h * 128 : (h + 1) * 128]
            v_l = okv[rows, 256 + h * 128 : 256 + (h + 1) * 128]
            s = dot(jnp.concatenate([k_l, k_cst[:128]], 1), qt[h, :, cols])
            pr = jnp.where(seen, jnp.exp2(s * EXP_SCALE), 0.0)
            dp = dot(jnp.concatenate([v_l, v_cst[:128]], 1), ct[h, :, cols])
            ds = (pr * dp).astype(BF)
            dqt[h, :, cols] = dot(k_l.T, ds)
            ok_st[side, :, h * 128 : (h + 1) * 128] = (dot(ds, qh[h, cols, :]) * SCALE).astype(BF)
            ok_st[side, :, 256 + h * 128 : 256 + (h + 1) * 128] = dot(pr.astype(BF), ch[h, cols, :]).astype(BF)

    for d in range(2):
        gather_wait(d, zs - 2)

    ok_out = []
    for j, out in enumerate((dok_out, dov_out)):
        lanes = slice(j * 256, (j + 1) * 256)
        ok_out.append(remote(ok_st.at[oc, :, lanes], half(out, core, 256), out_send.at[j], out_recv.at[j], sib))
        ok_out.append(pltpu.make_async_copy(ok_st.at[core, :, lanes], half(out, core, 256), out_sem.at[j]))
    for cp in ok_out:
        cp.start()

    def rs_copy(d, s):
        return remote(
            send_buf.at[d, s], recv_buf.at[d, s + 1], rs_send.at[d, s], rs_recv.at[d, s], ring_dst[d]
        )

    def step(s, carry):
        ids = [chunk_id(d, lax.rem(s + 1, zs)) for d in range(2)]
        k_aug = jnp.concatenate([kaug[ids[0]], kaug[ids[1]]], 0)
        for h in range(2):
            lanes = slice(h * 128, (h + 1) * 128)
            v_lanes = slice(256 + h * 128, 256 + (h + 1) * 128)
            k_l = jnp.concatenate([kv[ids[0], :, lanes], kv[ids[1], :, lanes]], 0)
            v_l = jnp.concatenate([kv[ids[0], :, v_lanes], kv[ids[1], :, v_lanes]], 0)
            k_full = jnp.concatenate([k_l, k_aug], 1)
            v_full = jnp.concatenate([v_l, v_cst], 1)
            k_t = k_l.T
            for n in range(4):
                cols = slice(n * 512, (n + 1) * 512)
                pr = jnp.exp2(dot(k_full, qt[h, :, cols]) * EXP_SCALE)
                dp = dot(v_full, ct[h, :, cols])
                ds = (pr * dp).astype(BF)
                p_s[:, cols] = pr.astype(BF)
                ds_s[:, cols] = ds
                dqt[h, :, cols] += dot(k_t, ds)
            dk = dot(ds_s[...], qh[h])
            dv = dot(p_s[...], ch[h])
            for d in range(2):
                fin[d, :, lanes] = dk[d * 128 : (d + 1) * 128]
                fin[d, :, v_lanes] = dv[d * 128 : (d + 1) * 128]

        @pl.when(s > 0)
        def _():
            for d in range(2):
                rs_copy(d, s - 1).wait_recv()

        for d in range(2):
            fin[d] = fin[d] + recv_buf[d, s].astype(F32)

        @pl.when(s < zs - 1)
        def _():
            for d in range(2):
                send_buf[d, s] = fin[d].astype(BF)
                rs_copy(d, s).start()

        return carry

    lax.fori_loop(0, zs, step, 0)

    fsend[...] = fin[...].astype(BF)
    me4 = yl * 2 + core
    f_out = [
        remote(
            fsend.at[yy, pl.ds(pl.multiple_of(kk * 64, 64), 64)],
            frecv.at[me4], f_send.at[i], f_recv.at[i], dev(p, yy, z, kk),
        )
        for i, (yy, kk) in enumerate(group)
    ]
    for cp in f_out:
        cp.start()
    frecv[me4] = fsend[yl, my_half, :]

    for h in range(2):
        for side in range(2):
            for g in range(GROUP):
                tile = dqt[h, :, tile_cols(side, g)] * SCALE
                dq_st[side, :, (h * 8 + g) * 128 : (h * 8 + g + 1) * 128] = tile.T.astype(BF)
    dq_copies = [
        remote(dq_st.at[oc], half(dq_out, core, 2048), out_send.at[2], out_recv.at[2], sib),
        pltpu.make_async_copy(dq_st.at[core], half(dq_out, core, 2048), out_sem.at[2]),
    ]
    for cp in dq_copies:
        cp.start()

    for cp in f_out:
        cp.wait_recv()
    for kk in range(2):
        tot = frecv[kk].astype(F32) + frecv[2 + kk].astype(F32)
        dpk_out[:, kk * 256 : (kk + 1) * 256] = tot[:, 0:256] * SCALE
        dpv_out[:, kk * 256 : (kk + 1) * 256] = tot[:, 256:512]

    for cp in ok_out + dq_copies:
        cp.wait()
    for cp in kv_out + cot_out + sib_out + f_out:
        cp.wait_send()

    def drain(t, carry):
        for d in range(2):
            gather(d, t).wait_send()
            rs_copy(d, t).wait_send()
        return carry

    lax.fori_loop(0, zs - 1, drain, 0)


def local(zs, pipes, q, o, g, ln, ok, ov, pk, pv, tab, lens):
    any_ = pl.BlockSpec(memory_space=pl.ANY)
    vmem = pl.BlockSpec(memory_space=pltpu.VMEM)
    smem = pl.BlockSpec(memory_space=pltpu.SMEM)
    chunks = 2 * zs
    blocks = chunks * 128 // BLK
    dma = pltpu.SemaphoreType.DMA
    outs = pl.pallas_call(
        functools.partial(kernel, zs, pipes),
        out_shape=(
            jax.ShapeDtypeStruct((ROWS, 4096), BF),
            jax.ShapeDtypeStruct((ROWS, 512), BF),
            jax.ShapeDtypeStruct((ROWS, 512), BF),
            jax.ShapeDtypeStruct((64, 512), F32),
            jax.ShapeDtypeStruct((64, 512), F32),
        ),
        in_specs=[any_, any_, any_, vmem, any_, any_, any_, any_, vmem, smem],
        out_specs=(any_, any_, any_, vmem, vmem),
        scratch_shapes=[
            pltpu.VMEM((256, 2048), BF),
            pltpu.VMEM((256, 2048), BF),
            pltpu.VMEM((256, 2048), BF),
            pltpu.VMEM((2, 2048, 128), BF),
            pltpu.VMEM((2, 2048, 128), BF),
            pltpu.VMEM((2, 256, 2048), BF),
            pltpu.VMEM((2, 256, 2048), BF),
            pltpu.VMEM((chunks, 128, 512), BF),
            pltpu.VMEM((chunks, 128, 128), BF),
            pltpu.VMEM((256, 512), BF),
            pltpu.VMEM((2, 128, 2048), F32),
            pltpu.VMEM((256, 2048), BF),
            pltpu.VMEM((256, 2048), BF),
            pltpu.VMEM((2, zs - 1, 128, 512), BF),
            pltpu.VMEM((2, zs, 128, 512), BF),
            pltpu.VMEM((2, 128, 512), F32),
            pltpu.VMEM((2, 128, 512), BF),
            pltpu.VMEM((4, 64, 512), BF),
            pltpu.VMEM((2, 128, 2048), BF),
            pltpu.VMEM((2, 128, 512), BF),
            pltpu.VMEM((32, 128), F32),
            pltpu.VMEM((2, 16, 128), F32),
            pltpu.VMEM((blocks, 128), F32),
            pltpu.VMEM((2, blocks, 128), F32),
            dma((6,)), dma((6,)), dma((6,)), dma((2, 2)), dma((2, 2)), dma((3, 2)), dma((3, 2)),
            dma((2, zs - 1)), dma((2, zs - 1)), dma((2, zs - 1)), dma((2, zs - 1)),
            dma((3,)), dma((3,)), dma((3,)), dma((3,)), dma((3,)),
        ],
        compiler_params=pltpu.CompilerParams(
            collective_id=0, has_side_effects=True, vmem_limit_bytes=50 * 1024 * 1024
        ),
    )(q[0], o[0], g[0], ln[0], ok[0], ov[0], pk[0], pv[0], tab[0], lens)
    return tuple(out[None] for out in outs)


def solution(mesh):
    rows = P("pipe", "ctx", None)
    in_specs = (rows,) * 9 + (P("pipe", "ctx"),)
    fn = functools.partial(local, mesh.shape["ctx"] // 4, mesh.shape["pipe"])
    return jax.shard_map(fn, mesh=mesh, in_specs=in_specs, out_specs=(rows,) * 5, check_vma=False)
```

```python
import functools
import math

import jax
import jax.numpy as jnp
from jax import lax
from jax.experimental import pallas as pl
from jax.experimental.pallas import tpu as pltpu
from jax.sharding import PartitionSpec as P

HD = 128
ROWS = 128
RLEN = 64
BLK = 32
GROUP = 8
SCALE = HD ** -0.5
EXP_SCALE = SCALE * math.log2(math.e)
FAR = 1e30
BF = jnp.bfloat16
F32 = jnp.float32
MESH = pl.DeviceIdType.MESH


def split3(x):
    hi = x.astype(BF).astype(F32)
    rest = x - hi
    mid = rest.astype(BF).astype(F32)
    return hi, mid, rest - mid


def dot(a, b):
    return jnp.dot(a, b, preferred_element_type=F32)


def kernel(
    zs, pipes,
    q_hbm, o_hbm, g_hbm, ln_ref, ok_hbm, ov_hbm, pk_hbm, pv_hbm, tab_ref, len_ref,
    dq_out, dok_out, dov_out, dpk_out, dpv_out,
    qb, ob, cb, qh, ch, qt, ct, kv, kaug, okv, dqt, ds_s, p_s, part,
    send_buf, recv_buf, fsend, frecv, dq_st, ok_st, ln_t, ln_r, bp_s, bp,
    loc_sem, sib_send, sib_recv, cot_send, cot_recv, kv_send, kv_recv,
    ga_send, ga_recv, rs_send, rs_recv, f_send, f_recv, out_sem, out_send, out_recv,
):
    p = lax.axis_index("pipe")
    c = lax.axis_index("ctx")
    core = lax.rem(c, 2)
    z = lax.rem(lax.div(c, 2), zs)
    yl = lax.div(c, 2 * zs)
    oc = 1 - core
    hops = zs // 2

    def dev(pp, yy, zz, kk):
        return (pp, (yy * zs + zz) * 2 + kk)

    sib = dev(p, yl, z, oc)
    z_up = lax.rem(z + 1, zs)
    z_dn = lax.rem(z + zs - 1, zs)
    p_up = lax.rem(p + 1, pipes)
    p_dn = lax.rem(p + pipes - 1, pipes)
    ring_dst = (dev(p, yl, z_up, core), dev(p, yl, z_dn, core))

    def lanes_at(ref, start, width):
        return ref.at[:, pl.ds(pl.multiple_of(start, 128), width)]

    def remote(src, dst, ss, rs, to):
        return pltpu.make_async_remote_copy(
            src_ref=src, dst_ref=dst, send_sem=ss, recv_sem=rs, device_id=to, device_id_type=MESH
        )

    my_rows = pl.ds(pl.multiple_of(core * ROWS, ROWS), ROWS)
    my_keys = pl.ds(pl.multiple_of(yl * 128 + core * 64, 64), 64)

    loc = [
        pltpu.make_async_copy(lanes_at(q_hbm, core * 2048, 2048), qb.at[my_rows], loc_sem.at[0]),
        pltpu.make_async_copy(lanes_at(o_hbm, core * 2048, 2048), ob.at[my_rows], loc_sem.at[1]),
        pltpu.make_async_copy(lanes_at(ok_hbm, core * 256, 256), okv.at[my_rows, 0:256], loc_sem.at[2]),
        pltpu.make_async_copy(lanes_at(ov_hbm, core * 256, 256), okv.at[my_rows, 256:512], loc_sem.at[3]),
    ]
    kv_loc = [
        [
            pltpu.make_async_copy(
                lanes_at(src, core * 256 + h * 128, 128),
                kv.at[h, z, my_keys, j * 128 : (j + 1) * 128],
                loc_sem.at[4 + 2 * h + j],
            )
            for j, src in enumerate((pk_hbm, pv_hbm))
        ]
        for h in range(2)
    ]
    for cp in kv_loc[0] + kv_loc[1] + loc:
        cp.start()

    row = lax.broadcasted_iota(jnp.int32, (32, ROWS), 1)
    length = jnp.where(row < RLEN, len_ref[0, 0], len_ref[0, 1])
    live = lax.rem(row, RLEN) < length
    ln_t[...] = jnp.where(live, ln_ref[...] * (1.0 / SCALE), FAR)
    lane = lax.broadcasted_iota(jnp.int32, bp_s.shape, 1)
    ids = lax.broadcasted_iota(jnp.int32, (bp_s.shape[0], tab_ref.shape[1]), 0)
    offs = jnp.zeros(bp_s.shape, F32)
    for rr in range(2):
        hit = jnp.where(tab_ref[rr : rr + 1, :] == ids, 1.0, 0.0)
        listed = jnp.max(hit, axis=1, keepdims=True)
        offs = jnp.where(lane == 3 + 2 * core + rr, (listed - 1.0) * FAR, offs)
    bp_s[...] = offs
    bp[core] = offs
    ln_r[core] = ln_t[pl.ds(pl.multiple_of(core * 16, 16), 16), :]

    barrier = pltpu.get_barrier_semaphore()
    partners = [
        sib,
        dev(p, 1 - yl, z, 0), dev(p, 1 - yl, z, 1),
        ring_dst[0], ring_dst[1],
        dev(p_dn, yl, z, 0), dev(p_dn, yl, z, 1),
        dev(p_up, yl, z, 0), dev(p_up, yl, z, 1),
    ]
    for to in partners:
        pl.semaphore_signal(barrier, inc=1, device_id=to, device_id_type=MESH)
    pl.semaphore_wait(barrier, len(partners))

    group = [(yl, oc), (1 - yl, core), (1 - yl, oc)]
    kv_out = [
        [
            remote(
                lanes_at(src, kk * 256 + h * 128, 128),
                kv.at[h, z, my_keys, j * 128 : (j + 1) * 128],
                kv_send.at[i, h, j], kv_recv.at[i, h, j], dev(p, yy, z, kk),
            )
            for i, (yy, kk) in enumerate(group)
            for j, src in enumerate((pk_hbm, pv_hbm))
        ]
        for h in range(2)
    ]
    for cp in kv_out[0] + kv_out[1]:
        cp.start()

    sib_out = [
        remote(lanes_at(q_hbm, oc * 2048, 2048), qb.at[my_rows], sib_send.at[0], sib_recv.at[0], sib),
        remote(lanes_at(o_hbm, oc * 2048, 2048), ob.at[my_rows], sib_send.at[1], sib_recv.at[1], sib),
        remote(lanes_at(ok_hbm, oc * 256, 256), okv.at[my_rows, 0:256], sib_send.at[2], sib_recv.at[2], sib),
        remote(lanes_at(ov_hbm, oc * 256, 256), okv.at[my_rows, 256:512], sib_send.at[3], sib_recv.at[3], sib),
        remote(ln_t.at[pl.ds(pl.multiple_of(oc * 16, 16), 16)], ln_r.at[core], sib_send.at[4], sib_recv.at[4], sib),
        remote(bp_s, bp.at[core], sib_send.at[5], sib_recv.at[5], sib),
    ]
    for i in (4, 5, 0, 2, 3, 1):
        sib_out[i].start()

    cot_out = [
        [
            remote(
                lanes_at(g_hbm, kk * 2048 + h * 1024, 1024),
                cb.at[my_rows, h * 1024 : (h + 1) * 1024],
                cot_send.at[h, d], cot_recv.at[h, d], dev(p_dn, yl, z, kk),
            )
            for d, kk in enumerate((oc, core))
        ]
        for h in range(2)
    ]

    def gather(h, d, t):
        chunk = lax.rem(z + zs - (t - 1), zs) if d == 0 else lax.rem(z + t - 1, zs)
        rows = slice(0, 256) if t < hops else slice(d * 128, (d + 1) * 128)
        ref = kv.at[h, chunk, rows]
        return remote(ref, ref, ga_send.at[h, d, t - 1], ga_recv.at[h, d, t - 1], ring_dst[d])

    def gather_wait(h, d, t):
        chunk = lax.rem(z + zs - t, zs) if d == 0 else lax.rem(z + t, zs)
        rows = slice(0, 256) if t < hops else slice(d * 128, (d + 1) * 128)
        ref = kv.at[h, chunk, rows]
        remote(ref, ref, ga_send.at[h, d, t - 1], ga_recv.at[h, d, t - 1], ring_dst[d]).wait_recv()

    def gather_pass(h, t):
        for d in range(2):
            gather_wait(h, d, t)
            if t < hops:
                gather(h, d, t + 1).start()

    for h in range(2):
        for cp in kv_loc[h]:
            cp.wait()
        for cp in kv_out[h]:
            cp.wait_recv()
        for d in range(2):
            gather(h, d, 1).start()
    for cp in cot_out[0]:
        cp.start()

    qt[:, 128:256, :] = jnp.zeros((2, 128, 2048), BF)
    ct[:, 128:256, :] = jnp.zeros((2, 128, 2048), BF)
    dqt[...] = jnp.zeros(dqt.shape, F32)
    sub = lax.broadcasted_iota(jnp.int32, (16, 128), 0)
    col = lax.broadcasted_iota(jnp.int32, (16, 128), 1)

    def tile_cols(side, g):
        return slice(side * 1024 + g * 128, side * 1024 + (g + 1) * 128)

    def query_tiles(h, side):
        for g in range(GROUP):
            cols = tile_cols(side, g)
            tile = qb[side * 128 : (side + 1) * 128, (h * 8 + g) * 128 : (h * 8 + g + 1) * 128]
            qh[h, cols, :] = tile
            qt[h, 0:128, cols] = tile.T
            hi, mid, low = split3(ln_r[side, h * 8 + g : h * 8 + g + 1, :])
            own = jnp.where(sub - 3 == side * 2 + lax.div(col, RLEN), 1.0, 0.0)
            aug = jnp.where(sub == 0, -hi, jnp.where(sub == 1, -mid, jnp.where(sub == 2, -low, own)))
            qt[h, 128:144, cols] = aug.astype(BF)

    def cot_tiles(h, side):
        for g in range(GROUP):
            cols = tile_cols(side, g)
            rows, lanes = slice(side * 128, (side + 1) * 128), slice((h * 8 + g) * 128, (h * 8 + g + 1) * 128)
            tile = cb[rows, lanes]
            ch[h, cols, :] = tile
            tile_t = tile.T
            ct[h, 0:128, cols] = tile_t
            prod = tile_t.astype(F32) * ob[rows, lanes].T.astype(F32)
            hi, mid, low = split3(jnp.sum(prod, axis=0, keepdims=True))
            aug = jnp.where(sub == 0, hi, jnp.where(sub == 1, mid, jnp.where(sub == 2, low, 0.0)))
            ct[h, 128:144, cols] = aug.astype(BF)

    sib_out[4].wait_recv()
    sib_out[5].wait_recv()
    aug_lane = lax.broadcasted_iota(jnp.int32, bp_s.shape, 1)
    blocks = bp[0] + bp[1] + jnp.where(aug_lane < 3, 1.0, 0.0)
    spread = jnp.broadcast_to(blocks[:, None, :], (blocks.shape[0], BLK, 128))
    spread = spread.reshape(2, zs, 128, 128).astype(BF)
    for yy in range(2):
        kaug[:, yy * 128 : (yy + 1) * 128, :] = spread[yy]

    def second_cot():
        for cp in cot_out[0]:
            cp.wait_send()
        for cp in cot_out[1]:
            cp.start()

    loc[0].wait()
    sib_out[0].wait_recv()
    for side in range(2):
        query_tiles(0, side)
    for t in range(1, hops - 1):
        gather_pass(0, t)
        if t == 1:
            for side in range(2):
                query_tiles(1, side)
        if t == hops - 2:
            second_cot()
        gather_pass(1, t)
    if hops < 3:
        for side in range(2):
            query_tiles(1, side)
        second_cot()

    loc[1].wait()
    for i in (1, 2, 3):
        sib_out[i].wait_recv()
    loc[2].wait()
    loc[3].wait()

    one_lane = lax.broadcasted_iota(jnp.int32, (256, 128), 1) < 3
    v_cst = jnp.where(one_lane, -1.0, 0.0).astype(BF)
    k_cst = jnp.where(one_lane, 1.0, 0.0).astype(BF)

    def own_part(h):
        key_i = lax.broadcasted_iota(jnp.int32, (ROWS, 1024), 0)
        row_i = lax.rem(lax.broadcasted_iota(jnp.int32, (ROWS, 1024), 1), ROWS)
        seen = (lax.div(key_i, RLEN) == lax.div(row_i, RLEN)) & (key_i <= row_i)
        for side in range(2):
            rows = slice(side * 128, (side + 1) * 128)
            cols = slice(side * 1024, (side + 1) * 1024)
            k_l = okv[rows, h * 128 : (h + 1) * 128]
            v_l = okv[rows, 256 + h * 128 : 256 + (h + 1) * 128]
            s = dot(jnp.concatenate([k_l, k_cst[:128]], 1), qt[h, :, cols])
            pr = jnp.where(seen, jnp.exp2(s * EXP_SCALE), 0.0)
            dp = dot(jnp.concatenate([v_l, v_cst[:128]], 1), ct[h, :, cols])
            ds = (pr * dp).astype(BF)
            dqt[h, :, cols] += dot(k_l.T, ds)
            ok_st[side, :, h * 128 : (h + 1) * 128] = (dot(ds, qh[h, cols, :]) * SCALE).astype(BF)
            ok_st[side, :, 256 + h * 128 : 256 + (h + 1) * 128] = dot(pr.astype(BF), ch[h, cols, :]).astype(BF)

    def unit(h, j):
        offset = lax.div(j + 1, 2) * (1 - 2 * lax.rem(j, 2))
        chunk = lax.rem(z + zs + offset, zs)
        k_l = kv[h, chunk, :, 0:128]
        k_full = jnp.concatenate([k_l, kaug[chunk]], 1)
        v_full = jnp.concatenate([kv[h, chunk, :, 128:256], v_cst], 1)
        for n in range(4):
            cols = slice(n * 512, (n + 1) * 512)
            pr = jnp.exp2(dot(k_full, qt[h, :, cols]) * EXP_SCALE)
            dp = dot(v_full, ct[h, :, cols])
            p_s[:, cols] = pr.astype(BF)
            ds_s[:, cols] = (pr * dp).astype(BF)
        dqt[h] += dot(k_l.T, ds_s[...])
        part[h, j, :, 0:128] = dot(ds_s[...], qh[h])
        part[h, j, :, 128:256] = dot(p_s[...], ch[h])

    def rs_rows(d, k):
        return slice(0, 256) if k < hops else slice(d * 128, (d + 1) * 128)

    def rs_copy(h, d, k):
        rows = rs_rows(d, k)
        return remote(
            send_buf.at[h, d, k - 1, rows], recv_buf.at[h, d, k - 1, rows],
            rs_send.at[h, d, k - 1], rs_recv.at[h, d, k - 1], ring_dst[d],
        )

    def rs_stage(h, d, k):
        j = zs - 1 if k == hops else (2 * k if d == 0 else 2 * k - 1)
        rows = rs_rows(d, k)
        send_buf[h, d, k - 1, rows] = part[h, j, rows].astype(BF)
        if k < hops:
            rs_copy(h, d, k + 1).wait_recv()
            got = rs_rows(d, k + 1)
            total = part[h, j, got] + recv_buf[h, d, k, got].astype(F32)
            send_buf[h, d, k - 1, got] = total.astype(BF)
        rs_copy(h, d, k).start()

    me4 = yl * 2 + core
    f_out = [
        [
            remote(
                fsend.at[h, pl.ds(pl.multiple_of(yy * 128 + kk * 64, 64), 64)],
                frecv.at[h, me4], f_send.at[h, i], f_recv.at[h, i], dev(p, yy, z, kk),
            )
            for i, (yy, kk) in enumerate(group)
        ]
        for h in range(2)
    ]

    def rs_last(h):
        total = part[h, 0]
        for d in range(2):
            rs_copy(h, d, 1).wait_recv()
            got = rs_rows(d, 1)
            if hops == 1:
                part[h, 0, got] += recv_buf[h, d, 0, got].astype(F32)
                total = part[h, 0]
            else:
                total = total + recv_buf[h, d, 0].astype(F32)
        fsend[h] = total.astype(BF)
        for cp in f_out[h]:
            cp.start()
        frecv[h, me4] = fsend[h, my_keys, :]

    def f_finish(h):
        for cp in f_out[h]:
            cp.wait_recv()
        for kk in range(2):
            tot = frecv[h, kk].astype(F32) + frecv[h, 2 + kk].astype(F32)
            lanes = slice((2 * kk + h) * 128, (2 * kk + h + 1) * 128)
            dpk_out[:, lanes] = tot[:, 0:128] * SCALE
            dpv_out[:, lanes] = tot[:, 128:256]

    def dq_tiles(h):
        for side in range(2):
            for g in range(GROUP):
                tile = dqt[h, :, tile_cols(side, g)] * SCALE
                dq_st[side, :, (h * 8 + g) * 128 : (h * 8 + g + 1) * 128] = tile.T.astype(BF)

    def dq_copies(h):
        lanes = slice(h * 1024, (h + 1) * 1024)
        dst = lanes_at(dq_out, core * 2048 + h * 1024, 1024)
        return [
            remote(dq_st.at[oc, :, lanes], dst, out_send.at[2 + h], out_recv.at[2 + h], sib),
            pltpu.make_async_copy(dq_st.at[core, :, lanes], dst, out_sem.at[2 + h]),
        ]

    for cp in cot_out[0]:
        cp.wait_recv()
    for side in range(2):
        cot_tiles(0, side)
    own_part(0)
    first = zs - 3

    def pass0(i, carry):
        late = jnp.minimum(lax.div(i, first), 1)
        j = (1 - late) * i + late * (first + lax.rem(i - first + 2 + 3 * zs, 3))

        @pl.when(i == first - 1)
        def _():
            for h in range(2):
                gather_pass(h, hops - 1)

        @pl.when(i == first)
        def _():
            gather_pass(0, hops)

        unit(0, j)

        @pl.when(i == first)
        def _():
            for d in range(2):
                rs_stage(0, d, hops)

        for d in range(2):
            @pl.when(i == zs - 1 - d)
            def _(d=d):
                rs_stage(0, d, hops - 1)

        return carry

    lax.fori_loop(0, zs, pass0, 0)

    gather_pass(1, hops)
    for cp in cot_out[1]:
        cp.wait_recv()
    for side in range(2):
        cot_tiles(1, side)

    def pass1(i, carry):
        unit(1, zs - 1 - i)

        @pl.when(i == 0)
        def _():
            for d in range(2):
                rs_stage(1, d, hops)

        for k in range(hops - 1, 0, -1):
            for d in range(2):
                @pl.when(i == 2 * (hops - k) - 1 + d)
                def _(d=d, k=k):
                    rs_stage(1, d, k)

            if k < hops - 1:
                @pl.when(i == 2 * (hops - 1 - k))
                def _(k=k):
                    for d in range(2):
                        rs_stage(0, d, k)

        return carry

    lax.fori_loop(0, zs, pass1, 0)

    rs_last(0)
    own_part(1)
    ok_out = []
    for j, out in enumerate((dok_out, dov_out)):
        lanes = slice(j * 256, (j + 1) * 256)
        dst = lanes_at(out, core * 256, 256)
        ok_out.append(remote(ok_st.at[oc, :, lanes], dst, out_send.at[j], out_recv.at[j], sib))
        ok_out.append(pltpu.make_async_copy(ok_st.at[core, :, lanes], dst, out_sem.at[j]))
    for cp in ok_out:
        cp.start()
    for h in range(2):
        dq_tiles(h)
        for cp in dq_copies(h):
            cp.start()
    rs_last(1)
    f_finish(0)
    for cp in ok_out + dq_copies(0) + dq_copies(1):
        cp.wait()
    for cp in kv_out[0] + kv_out[1] + cot_out[1] + sib_out + f_out[0]:
        cp.wait_send()
    for h in range(2):
        for d in range(2):
            for t in range(1, hops + 1):
                gather(h, d, t).wait_send()
                rs_copy(h, d, t).wait_send()
    f_finish(1)
    for cp in f_out[1]:
        cp.wait_send()


def hand_over(*refs):
    for src, dst in zip(refs[:5], refs[5:]):
        dst[...] = src[...]


def local(zs, pipes, q, o, g, ln, ok, ov, pk, pv, tab, lens):
    any_ = pl.BlockSpec(memory_space=pl.ANY)
    vmem = pl.BlockSpec(memory_space=pltpu.VMEM)
    smem = pl.BlockSpec(memory_space=pltpu.SMEM)
    hops = zs // 2
    blocks = zs * 256 // BLK
    dma = pltpu.SemaphoreType.DMA
    outs = pl.pallas_call(
        functools.partial(kernel, zs, pipes),
        out_shape=(
            jax.ShapeDtypeStruct((ROWS, 4096), BF),
            jax.ShapeDtypeStruct((ROWS, 512), BF),
            jax.ShapeDtypeStruct((ROWS, 512), BF),
            jax.ShapeDtypeStruct((64, 512), F32),
            jax.ShapeDtypeStruct((64, 512), F32),
        ),
        in_specs=[any_, any_, any_, vmem, any_, any_, any_, any_, vmem, smem],
        out_specs=(any_, any_, any_, vmem, vmem),
        scratch_shapes=[
            pltpu.VMEM((256, 2048), BF),
            pltpu.VMEM((256, 2048), BF),
            pltpu.VMEM((256, 2048), BF),
            pltpu.VMEM((2, 2048, 128), BF),
            pltpu.VMEM((2, 2048, 128), BF),
            pltpu.VMEM((2, 256, 2048), BF),
            pltpu.VMEM((2, 256, 2048), BF),
            pltpu.VMEM((2, zs, 256, 256), BF),
            pltpu.VMEM((zs, 256, 128), BF),
            pltpu.VMEM((256, 512), BF),
            pltpu.VMEM((2, 128, 2048), F32),
            pltpu.VMEM((256, 2048), BF),
            pltpu.VMEM((256, 2048), BF),
            pltpu.VMEM((2, zs, 256, 256), F32),
            pltpu.VMEM((2, 2, hops, 256, 256), BF),
            pltpu.VMEM((2, 2, hops, 256, 256), BF),
            pltpu.VMEM((2, 256, 256), BF),
            pltpu.VMEM((2, 4, 64, 256), BF),
            pltpu.VMEM((2, 128, 2048), BF),
            pltpu.VMEM((2, 128, 512), BF),
            pltpu.VMEM((32, 128), F32),
            pltpu.VMEM((2, 16, 128), F32),
            pltpu.VMEM((blocks, 128), F32),
            pltpu.VMEM((2, blocks, 128), F32),
            dma((8,)), dma((6,)), dma((6,)), dma((2, 2)), dma((2, 2)), dma((3, 2, 2)), dma((3, 2, 2)),
            dma((2, 2, hops)), dma((2, 2, hops)), dma((2, 2, hops)), dma((2, 2, hops)),
            dma((2, 3)), dma((2, 3)), dma((4,)), dma((4,)), dma((4,)),
        ],
        compiler_params=pltpu.CompilerParams(
            collective_id=0, has_side_effects=True, vmem_limit_bytes=56 * 1024 * 1024
        ),
    )(q[0], o[0], g[0], ln[0].T, ok[0], ov[0], pk[0], pv[0], tab[0], lens)
    outs = pl.pallas_call(
        hand_over,
        out_shape=tuple(jax.ShapeDtypeStruct(out.shape, out.dtype) for out in outs),
        in_specs=[vmem] * 5,
        out_specs=(vmem,) * 5,
    )(*outs)
    return tuple(out[None] for out in outs)


def solution(mesh):
    rows = P("pipe", "ctx", None)
    in_specs = (rows,) * 9 + (P("pipe", "ctx"),)
    fn = functools.partial(local, mesh.shape["ctx"] // 4, mesh.shape["pipe"])
    return jax.shard_map(fn, mesh=mesh, in_specs=in_specs, out_specs=(rows,) * 5, check_vma=False)
```

```python
import functools
import math

import jax
import jax.numpy as jnp
from jax import lax
from jax.experimental import pallas as pl
from jax.experimental.pallas import tpu as pltpu
from jax.sharding import PartitionSpec as P

HD = 128
ROWS = 128
RLEN = 64
BLK = 32
GROUP = 8
SCALE = HD ** -0.5
EXP_SCALE = SCALE * math.log2(math.e)
FAR = 1e30
BF = jnp.bfloat16
F32 = jnp.float32
MESH = pl.DeviceIdType.MESH


def split3(x):
    hi = x.astype(BF).astype(F32)
    rest = x - hi
    mid = rest.astype(BF).astype(F32)
    return hi, mid, rest - mid


def dot(a, b):
    return jnp.dot(a, b, preferred_element_type=F32)


def kernel(
    zs, pipes,
    q_hbm, o_hbm, g_hbm, ln_ref, ok_hbm, ov_hbm, pk_hbm, pv_hbm, tab_ref, len_ref,
    dq_out, dok_out, dov_out, dpk_out, dpv_out,
    qb, ob, cb, qh, ch, qt, ct, kv, kaug, okv, dqt, ds_s, p_s, part,
    send_buf, recv_buf, y_buf, y_got, z_buf, z_got, fsend, frecv, fsum, fgot, dq_st, ok_st, ln_t, ln_r, bp_s, bp,
    loc_sem, sib_send, sib_recv, cot_send, cot_recv, kv_send, kv_recv,
    ga_send, ga_recv, rs_send, rs_recv, y_send, y_recv, z_send, z_recv, f_send, f_recv, out_sem, out_send, out_recv,
):
    p = lax.axis_index("pipe")
    c = lax.axis_index("ctx")
    core = lax.rem(c, 2)
    z = lax.rem(lax.div(c, 2), zs)
    yl = lax.div(c, 2 * zs)
    oc = 1 - core
    hops = zs // 2

    def dev(pp, yy, zz, kk):
        return (pp, (yy * zs + zz) * 2 + kk)

    sib = dev(p, yl, z, oc)
    z_up = lax.rem(z + 1, zs)
    z_dn = lax.rem(z + zs - 1, zs)
    p_up = lax.rem(p + 1, pipes)
    p_dn = lax.rem(p + pipes - 1, pipes)
    ring_dst = (dev(p, yl, z_up, core), dev(p, yl, z_dn, core))

    def lanes_at(ref, start, width):
        return ref.at[:, pl.ds(pl.multiple_of(start, 128), width)]

    def remote(src, dst, ss, rs, to):
        return pltpu.make_async_remote_copy(
            src_ref=src, dst_ref=dst, send_sem=ss, recv_sem=rs, device_id=to, device_id_type=MESH
        )

    my_rows = pl.ds(pl.multiple_of(core * ROWS, ROWS), ROWS)
    my_keys = pl.ds(pl.multiple_of(yl * 128 + core * 64, 64), 64)

    loc = [
        pltpu.make_async_copy(lanes_at(q_hbm, core * 2048, 2048), qb.at[my_rows], loc_sem.at[0]),
        pltpu.make_async_copy(lanes_at(o_hbm, core * 2048, 2048), ob.at[my_rows], loc_sem.at[1]),
        pltpu.make_async_copy(lanes_at(ok_hbm, core * 256, 256), okv.at[my_rows, 0:256], loc_sem.at[2]),
        pltpu.make_async_copy(lanes_at(ov_hbm, core * 256, 256), okv.at[my_rows, 256:512], loc_sem.at[3]),
    ]
    kv_loc = [
        [
            pltpu.make_async_copy(
                lanes_at(src, core * 256 + h * 128, 128),
                kv.at[h, z, my_keys, j * 128 : (j + 1) * 128],
                loc_sem.at[4 + 2 * h + j],
            )
            for j, src in enumerate((pk_hbm, pv_hbm))
        ]
        for h in range(2)
    ]
    for cp in kv_loc[0] + kv_loc[1] + loc:
        cp.start()

    row = lax.broadcasted_iota(jnp.int32, (32, ROWS), 1)
    length = jnp.where(row < RLEN, len_ref[0, 0], len_ref[0, 1])
    live = lax.rem(row, RLEN) < length
    ln_t[...] = jnp.where(live, ln_ref[...] * (1.0 / SCALE), FAR)
    lane = lax.broadcasted_iota(jnp.int32, bp_s.shape, 1)
    ids = lax.broadcasted_iota(jnp.int32, (bp_s.shape[0], tab_ref.shape[1]), 0)
    offs = jnp.zeros(bp_s.shape, F32)
    for rr in range(2):
        hit = jnp.where(tab_ref[rr : rr + 1, :] == ids, 1.0, 0.0)
        listed = jnp.max(hit, axis=1, keepdims=True)
        offs = jnp.where(lane == 3 + 2 * core + rr, (listed - 1.0) * FAR, offs)
    bp_s[...] = offs
    bp[core] = offs
    ln_r[core] = ln_t[pl.ds(pl.multiple_of(core * 16, 16), 16), :]

    barrier = pltpu.get_barrier_semaphore()
    partners = [
        sib,
        dev(p, 1 - yl, z, 0), dev(p, 1 - yl, z, 1),
        ring_dst[0], ring_dst[1],
        dev(p_dn, yl, z, 0), dev(p_dn, yl, z, 1),
        dev(p_up, yl, z, 0), dev(p_up, yl, z, 1),
    ]
    for to in partners:
        pl.semaphore_signal(barrier, inc=1, device_id=to, device_id_type=MESH)
    pl.semaphore_wait(barrier, len(partners))

    group = [(yl, oc), (1 - yl, core), (1 - yl, oc)]
    kv_out = [
        [
            remote(
                lanes_at(src, kk * 256 + h * 128, 128),
                kv.at[h, z, my_keys, j * 128 : (j + 1) * 128],
                kv_send.at[i, h, j], kv_recv.at[i, h, j], dev(p, yy, z, kk),
            )
            for i, (yy, kk) in enumerate(group)
            for j, src in enumerate((pk_hbm, pv_hbm))
        ]
        for h in range(2)
    ]
    for cp in kv_out[0] + kv_out[1]:
        cp.start()

    sib_out = [
        remote(lanes_at(q_hbm, oc * 2048, 2048), qb.at[my_rows], sib_send.at[0], sib_recv.at[0], sib),
        remote(lanes_at(o_hbm, oc * 2048, 2048), ob.at[my_rows], sib_send.at[1], sib_recv.at[1], sib),
        remote(lanes_at(ok_hbm, oc * 256, 256), okv.at[my_rows, 0:256], sib_send.at[2], sib_recv.at[2], sib),
        remote(lanes_at(ov_hbm, oc * 256, 256), okv.at[my_rows, 256:512], sib_send.at[3], sib_recv.at[3], sib),
        remote(ln_t.at[pl.ds(pl.multiple_of(oc * 16, 16), 16)], ln_r.at[core], sib_send.at[4], sib_recv.at[4], sib),
        remote(bp_s, bp.at[core], sib_send.at[5], sib_recv.at[5], sib),
    ]
    for i in (4, 5, 0, 2, 3, 1):
        sib_out[i].start()

    cot_out = [
        [
            remote(
                lanes_at(g_hbm, kk * 2048 + part_i * 512, 512),
                cb.at[my_rows, part_i * 512 : (part_i + 1) * 512],
                cot_send.at[part_i, d], cot_recv.at[part_i, d], dev(p_dn, yl, z, kk),
            )
            for d, kk in enumerate((oc, core))
        ]
        for part_i in range(4)
    ]

    def cot_next(done):
        for cp in cot_out[done]:
            cp.wait_send()
        for cp in cot_out[done + 1]:
            cp.start()

    def cot_wait(i):
        for cp in cot_out[i]:
            cp.wait_recv()

    def gather(h, d, t):
        chunk = lax.rem(z + zs - (t - 1), zs) if d == 0 else lax.rem(z + t - 1, zs)
        rows = slice(0, 256) if t < hops else slice(d * 128, (d + 1) * 128)
        ref = kv.at[h, chunk, rows]
        return remote(ref, ref, ga_send.at[h, d, t - 1], ga_recv.at[h, d, t - 1], ring_dst[d])

    def gather_wait(h, d, t):
        chunk = lax.rem(z + zs - t, zs) if d == 0 else lax.rem(z + t, zs)
        rows = slice(0, 256) if t < hops else slice(d * 128, (d + 1) * 128)
        ref = kv.at[h, chunk, rows]
        remote(ref, ref, ga_send.at[h, d, t - 1], ga_recv.at[h, d, t - 1], ring_dst[d]).wait_recv()

    def gather_pass(h, t):
        for d in range(2):
            gather_wait(h, d, t)
            if t < hops:
                gather(h, d, t + 1).start()

    for h in range(2):
        for cp in kv_loc[h]:
            cp.wait()
        for cp in kv_out[h]:
            cp.wait_recv()
        for d in range(2):
            gather(h, d, 1).start()
    for cp in cot_out[0]:
        cp.start()

    qt[:, 128:256, :] = jnp.zeros((2, 128, 2048), BF)
    ct[:, 128:256, :] = jnp.zeros((2, 128, 2048), BF)
    dqt[...] = jnp.zeros(dqt.shape, F32)
    sub = lax.broadcasted_iota(jnp.int32, (16, 128), 0)
    col = lax.broadcasted_iota(jnp.int32, (16, 128), 1)

    def tile_cols(side, g):
        start = (g // 4) * 1024 + side * 512 + (g % 4) * 128
        return slice(start, start + 128)

    def query_tiles(h, side):
        for g in range(GROUP):
            cols = tile_cols(side, g)
            tile = qb[side * 128 : (side + 1) * 128, (h * 8 + g) * 128 : (h * 8 + g + 1) * 128]
            qh[h, cols, :] = tile
            qt[h, 0:128, cols] = tile.T
            hi, mid, low = split3(ln_r[side, h * 8 + g : h * 8 + g + 1, :])
            own = jnp.where(sub - 3 == side * 2 + lax.div(col, RLEN), 1.0, 0.0)
            aug = jnp.where(sub == 0, -hi, jnp.where(sub == 1, -mid, jnp.where(sub == 2, -low, own)))
            qt[h, 128:144, cols] = aug.astype(BF)

    def cot_tiles(h, q):
        for side, g in [(side, g) for side in range(2) for g in range(q * 4, q * 4 + 4)]:
            cols = tile_cols(side, g)
            rows, lanes = slice(side * 128, (side + 1) * 128), slice((h * 8 + g) * 128, (h * 8 + g + 1) * 128)
            tile = cb[rows, lanes]
            ch[h, cols, :] = tile
            tile_t = tile.T
            ct[h, 0:128, cols] = tile_t
            prod = tile_t.astype(F32) * ob[rows, lanes].T.astype(F32)
            hi, mid, low = split3(jnp.sum(prod, axis=0, keepdims=True))
            aug = jnp.where(sub == 0, hi, jnp.where(sub == 1, mid, jnp.where(sub == 2, low, 0.0)))
            ct[h, 128:144, cols] = aug.astype(BF)

    sib_out[4].wait_recv()
    sib_out[5].wait_recv()
    aug_lane = lax.broadcasted_iota(jnp.int32, bp_s.shape, 1)
    blocks = bp[0] + bp[1] + jnp.where(aug_lane < 3, 1.0, 0.0)
    spread = jnp.broadcast_to(blocks[:, None, :], (blocks.shape[0], BLK, 128))
    spread = spread.reshape(2, zs, 128, 128).astype(BF)
    for yy in range(2):
        kaug[:, yy * 128 : (yy + 1) * 128, :] = spread[yy]

    loc[0].wait()
    sib_out[0].wait_recv()
    for side in range(2):
        query_tiles(0, side)
    if hops > 2:
        gather_pass(0, 1)
    for side in range(2):
        query_tiles(1, side)
    cot_next(0)
    if hops > 2:
        gather_pass(1, 1)

    loc[1].wait()
    for i in (1, 2, 3):
        sib_out[i].wait_recv()
    loc[2].wait()
    loc[3].wait()

    one_lane = lax.broadcasted_iota(jnp.int32, (256, 128), 1) < 3
    v_cst = jnp.where(one_lane, -1.0, 0.0).astype(BF)
    k_cst = jnp.where(one_lane, 1.0, 0.0).astype(BF)

    def own_part(h):
        key_i = lax.broadcasted_iota(jnp.int32, (ROWS, 512), 0)
        row_i = lax.rem(lax.broadcasted_iota(jnp.int32, (ROWS, 512), 1), ROWS)
        seen = (lax.div(key_i, RLEN) == lax.div(row_i, RLEN)) & (key_i <= row_i)
        for side in range(2):
            rows = slice(side * 128, (side + 1) * 128)
            k_l = okv[rows, h * 128 : (h + 1) * 128]
            v_l = okv[rows, 256 + h * 128 : 256 + (h + 1) * 128]
            k_full = jnp.concatenate([k_l, k_cst[:128]], 1)
            v_full = jnp.concatenate([v_l, v_cst[:128]], 1)
            dk = jnp.zeros((ROWS, HD), F32)
            dv = jnp.zeros((ROWS, HD), F32)
            for q in range(2):
                cols = slice(q * 1024 + side * 512, q * 1024 + (side + 1) * 512)
                pr = jnp.where(seen, jnp.exp2(dot(k_full, qt[h, :, cols]) * EXP_SCALE), 0.0)
                ds = (pr * dot(v_full, ct[h, :, cols])).astype(BF)
                dqt[h, :, cols] += dot(k_l.T, ds)
                dk += dot(ds, qh[h, cols, :])
                dv += dot(pr.astype(BF), ch[h, cols, :])
            ok_st[side, :, h * 128 : (h + 1) * 128] = (dk * SCALE).astype(BF)
            ok_st[side, :, 256 + h * 128 : 256 + (h + 1) * 128] = dv.astype(BF)

    def unit(h, j, q=None):
        lo, hi = (0, 2048) if q is None else (q * 1024, (q + 1) * 1024)
        offset = lax.div(j + 1, 2) * (1 - 2 * lax.rem(j, 2))
        chunk = lax.rem(z + zs + offset, zs)
        k_l = kv[h, chunk, :, 0:128]
        k_full = jnp.concatenate([k_l, kaug[chunk]], 1)
        v_full = jnp.concatenate([kv[h, chunk, :, 128:256], v_cst], 1)
        for n in range(lo, hi, 512):
            cols = slice(n, n + 512)
            pr = jnp.exp2(dot(k_full, qt[h, :, cols]) * EXP_SCALE)
            dp = dot(v_full, ct[h, :, cols])
            p_s[:, cols] = pr.astype(BF)
            ds_s[:, cols] = (pr * dp).astype(BF)
        dqt[h, :, lo:hi] += dot(k_l.T, ds_s[:, lo:hi])
        dk = dot(ds_s[:, lo:hi], qh[h, lo:hi])
        dv = dot(p_s[:, lo:hi], ch[h, lo:hi])
        if q == 1:
            part[h, j, :, 0:128] += dk
            part[h, j, :, 128:256] += dv
        else:
            part[h, j, :, 0:128] = dk
            part[h, j, :, 128:256] = dv

    def rs_rows(d, k):
        return slice(0, 256) if k < hops else slice(d * 128, (d + 1) * 128)

    def place(d, k):
        return zs - 1 if k == hops else (2 * k if d == 0 else 2 * k - 1)

    def rs_copy(d, k):
        rows = rs_rows(d, k)
        return remote(
            send_buf.at[d, k - 1, rows], recv_buf.at[d, k - 1, rows],
            rs_send.at[d, k - 1], rs_recv.at[d, k - 1], ring_dst[d],
        )

    def rs_stage(d, k):
        j = place(d, k)
        rows = rs_rows(d, k)
        send_buf[d, k - 1, rows] = part[0, j, rows].astype(BF)
        if k < hops:
            rs_copy(d, k + 1).wait_recv()
            got = rs_rows(d, k + 1)
            total = part[0, j, got] + recv_buf[d, k, got].astype(F32)
            send_buf[d, k - 1, got] = total.astype(BF)
        rs_copy(d, k).start()

    me4 = yl * 2 + core
    f_out = [
        remote(
            fsend.at[pl.ds(pl.multiple_of(yy * 128 + kk * 64, 64), 64)],
            frecv.at[me4], f_send.at[i], f_recv.at[i], dev(p, yy, z, kk),
        )
        for i, (yy, kk) in enumerate(group)
    ]

    def rs_last():
        for d in range(2):
            rs_copy(d, 1).wait_recv()
            got = rs_rows(d, 1)
            part[0, 0, got] += recv_buf[d, 0, got].astype(F32)
        fsend[...] = part[0, 0].astype(BF)
        for cp in f_out:
            cp.start()
        frecv[me4] = fsend[my_keys, :]

    def pool_out(h, kk, tot):
        lanes = slice((2 * kk + h) * 128, (2 * kk + h + 1) * 128)
        dpk_out[:, lanes] = tot[:, 0:128] * SCALE
        dpv_out[:, lanes] = tot[:, 128:256]

    def rs_finish():
        for cp in f_out:
            cp.wait_recv()
        for kk in range(2):
            pool_out(0, kk, frecv[kk].astype(F32) + frecv[2 + kk].astype(F32))

    def y_copy(j):
        return remote(y_buf.at[j], y_got.at[j], y_send.at[j], y_recv.at[j], dev(p, 1 - yl, z, core))

    def own_rows(rows):
        return pl.ds(pl.multiple_of(yl * 128 + rows.start, 64), rows.stop - rows.start)

    def y_start(j):
        other = pl.ds(pl.multiple_of((1 - yl) * 128, 128), 128)
        y_buf[j] = part[1, j, other].astype(BF)
        y_copy(j).start()

    def y_add(j):
        y_copy(j).wait_recv()
        mine = own_rows(slice(0, 128))
        part[1, j, mine] = part[1, j, mine] + y_got[j].astype(F32)

    def z_rows(d, k):
        return slice(0, 128) if k < hops else slice(d * 64, (d + 1) * 64)

    def z_copy(d, k):
        rows = z_rows(d, k)
        return remote(
            z_buf.at[d, k - 1, rows], z_got.at[d, k - 1, rows],
            z_send.at[d, k - 1], z_recv.at[d, k - 1], ring_dst[d],
        )

    def z_stage(d, k):
        j = place(d, k)
        rows = z_rows(d, k)
        if k < hops or d == 0:
            y_add(j)
        z_buf[d, k - 1, rows] = part[1, j, own_rows(rows)].astype(BF)
        if k < hops:
            z_copy(d, k + 1).wait_recv()
            got = z_rows(d, k + 1)
            total = part[1, j, own_rows(got)] + z_got[d, k, got].astype(F32)
            z_buf[d, k - 1, got] = total.astype(BF)
        z_copy(d, k).start()

    sum_out = remote(
        fsum.at[pl.ds(pl.multiple_of(oc * 64, 64), 64)], fgot.at[core], f_send.at[3], f_recv.at[3], sib
    )

    def z_last():
        y_add(0)
        fsum[...] = part[1, 0, own_rows(slice(0, 128))]
        for d in range(2):
            z_copy(d, 1).wait_recv()
            got = z_rows(d, 1)
            fsum[got] += z_got[d, 0, got].astype(F32)
        sum_out.start()
        fgot[core] = fsum[pl.ds(pl.multiple_of(core * 64, 64), 64), :]

    def z_finish():
        sum_out.wait_recv()
        for kk in range(2):
            pool_out(1, kk, fgot[kk])

    def dq_tiles(h):
        for side in range(2):
            for g in range(GROUP):
                tile = dqt[h, :, tile_cols(side, g)] * SCALE
                dq_st[side, :, (h * 8 + g) * 128 : (h * 8 + g + 1) * 128] = tile.T.astype(BF)

    def dq_copies(h):
        lanes = slice(h * 1024, (h + 1) * 1024)
        dst = lanes_at(dq_out, core * 2048 + h * 1024, 1024)
        return [
            remote(dq_st.at[oc, :, lanes], dst, out_send.at[2 + h], out_recv.at[2 + h], sib),
            pltpu.make_async_copy(dq_st.at[core, :, lanes], dst, out_sem.at[2 + h]),
        ]

    near = zs - 3
    cot_wait(0)
    cot_tiles(0, 0)

    def near_first(j, carry):
        if hops > 3:
            @pl.when(j == 3)
            def _():
                gather_pass(0, 2)

        unit(0, j, 0)
        return carry

    def near_second(j, carry):
        unit(0, j, 1)
        return carry

    def far(i, carry):
        unit(0, near + lax.rem(i + 2, 3))

        @pl.when(i == 0)
        def _():
            for d in range(2):
                rs_stage(d, hops)

        return carry

    lax.fori_loop(0, near, near_first, 0)
    if hops > 3:
        gather_pass(1, 2)
    cot_next(1)
    cot_wait(1)
    cot_tiles(0, 1)
    lax.fori_loop(0, near, near_second, 0)
    own_part(0)
    for h in range(2):
        gather_pass(h, hops - 1)
    cot_next(2)
    gather_pass(0, hops)
    lax.fori_loop(0, 3, far, 0)
    for d in range(2):
        rs_stage(d, hops - 1)
    dq_tiles(0)
    for cp in dq_copies(0):
        cp.start()

    gather_pass(1, hops)
    for q in range(2):
        cot_wait(2 + q)
        cot_tiles(1, q)

    def pass1(i, carry):
        unit(1, zs - 1 - i)
        y_start(zs - 1 - i)

        @pl.when(i == 2)
        def _():
            for d in range(2):
                z_stage(d, hops)
            for d in range(2):
                if hops > 2:
                    rs_stage(d, hops - 2)

        for k in range(hops - 1, 1, -1):
            @pl.when(i == 2 * (hops - k) + 2)
            def _(k=k):
                for d in range(2):
                    z_stage(d, k)

        if hops > 3:
            @pl.when(i == zs - 3)
            def _():
                for d in range(2):
                    rs_stage(d, hops - 3)

        return carry

    lax.fori_loop(0, zs, pass1, 0)

    own_part(1)
    ok_out = []
    for j, out in enumerate((dok_out, dov_out)):
        lanes = slice(j * 256, (j + 1) * 256)
        dst = lanes_at(out, core * 256, 256)
        ok_out.append(remote(ok_st.at[oc, :, lanes], dst, out_send.at[j], out_recv.at[j], sib))
        ok_out.append(pltpu.make_async_copy(ok_st.at[core, :, lanes], dst, out_sem.at[j]))
    for cp in ok_out:
        cp.start()
    rs_last()
    for d in range(2):
        z_stage(d, 1)
    dq_tiles(1)
    for cp in dq_copies(1):
        cp.start()
    rs_finish()
    z_last()
    for cp in ok_out + dq_copies(0) + dq_copies(1):
        cp.wait()
    for cp in kv_out[0] + kv_out[1] + cot_out[3] + sib_out + f_out:
        cp.wait_send()
    for d in range(2):
        for t in range(1, hops + 1):
            for h in range(2):
                gather(h, d, t).wait_send()
            rs_copy(d, t).wait_send()
            z_copy(d, t).wait_send()
    for j in range(zs):
        y_copy(j).wait_send()
    z_finish()
    sum_out.wait_send()


def hand_over(*refs):
    for src, dst in zip(refs[:5], refs[5:]):
        dst[...] = src[...]


def local(zs, pipes, q, o, g, ln, ok, ov, pk, pv, tab, lens):
    any_ = pl.BlockSpec(memory_space=pl.ANY)
    vmem = pl.BlockSpec(memory_space=pltpu.VMEM)
    smem = pl.BlockSpec(memory_space=pltpu.SMEM)
    hops = zs // 2
    blocks = zs * 256 // BLK
    dma = pltpu.SemaphoreType.DMA
    outs = pl.pallas_call(
        functools.partial(kernel, zs, pipes),
        out_shape=(
            jax.ShapeDtypeStruct((ROWS, 4096), BF),
            jax.ShapeDtypeStruct((ROWS, 512), BF),
            jax.ShapeDtypeStruct((ROWS, 512), BF),
            jax.ShapeDtypeStruct((64, 512), F32),
            jax.ShapeDtypeStruct((64, 512), F32),
        ),
        in_specs=[any_, any_, any_, vmem, any_, any_, any_, any_, vmem, smem],
        out_specs=(any_, any_, any_, vmem, vmem),
        scratch_shapes=[
            pltpu.VMEM((256, 2048), BF),
            pltpu.VMEM((256, 2048), BF),
            pltpu.VMEM((256, 2048), BF),
            pltpu.VMEM((2, 2048, 128), BF),
            pltpu.VMEM((2, 2048, 128), BF),
            pltpu.VMEM((2, 256, 2048), BF),
            pltpu.VMEM((2, 256, 2048), BF),
            pltpu.VMEM((2, zs, 256, 256), BF),
            pltpu.VMEM((zs, 256, 128), BF),
            pltpu.VMEM((256, 512), BF),
            pltpu.VMEM((2, 128, 2048), F32),
            pltpu.VMEM((256, 2048), BF),
            pltpu.VMEM((256, 2048), BF),
            pltpu.VMEM((2, zs, 256, 256), F32),
            pltpu.VMEM((2, hops, 256, 256), BF),
            pltpu.VMEM((2, hops, 256, 256), BF),
            pltpu.VMEM((zs, 128, 256), BF),
            pltpu.VMEM((zs, 128, 256), BF),
            pltpu.VMEM((2, hops, 128, 256), BF),
            pltpu.VMEM((2, hops, 128, 256), BF),
            pltpu.VMEM((256, 256), BF),
            pltpu.VMEM((4, 64, 256), BF),
            pltpu.VMEM((128, 256), F32),
            pltpu.VMEM((2, 64, 256), F32),
            pltpu.VMEM((2, 128, 2048), BF),
            pltpu.VMEM((2, 128, 512), BF),
            pltpu.VMEM((32, 128), F32),
            pltpu.VMEM((2, 16, 128), F32),
            pltpu.VMEM((blocks, 128), F32),
            pltpu.VMEM((2, blocks, 128), F32),
            dma((8,)), dma((6,)), dma((6,)), dma((4, 2)), dma((4, 2)), dma((3, 2, 2)), dma((3, 2, 2)),
            dma((2, 2, hops)), dma((2, 2, hops)), dma((2, hops)), dma((2, hops)),
            dma((zs,)), dma((zs,)), dma((2, hops)), dma((2, hops)),
            dma((4,)), dma((4,)), dma((4,)), dma((4,)), dma((4,)),
        ],
        compiler_params=pltpu.CompilerParams(
            collective_id=0, has_side_effects=True, vmem_limit_bytes=56 * 1024 * 1024
        ),
    )(q[0], o[0], g[0], ln[0].T, ok[0], ov[0], pk[0], pv[0], tab[0], lens)
    outs = pl.pallas_call(
        hand_over,
        out_shape=tuple(jax.ShapeDtypeStruct(out.shape, out.dtype) for out in outs),
        in_specs=[vmem] * 5,
        out_specs=(vmem,) * 5,
    )(*outs)
    return tuple(out[None] for out in outs)


def solution(mesh):
    rows = P("pipe", "ctx", None)
    in_specs = (rows,) * 9 + (P("pipe", "ctx"),)
    fn = functools.partial(local, mesh.shape["ctx"] // 4, mesh.shape["pipe"])
    return jax.shard_map(fn, mesh=mesh, in_specs=in_specs, out_specs=(rows,) * 5, check_vma=False)
```

```python
import functools
import math

import jax
import jax.numpy as jnp
from jax import lax
from jax.experimental import pallas as pl
from jax.experimental.pallas import tpu as pltpu
from jax.sharding import PartitionSpec as P

HD = 128
ROWS = 128
RLEN = 64
BLK = 32
GROUP = 8
SCALE = HD ** -0.5
EXP_SCALE = SCALE * math.log2(math.e)
FAR = 1e30
BF = jnp.bfloat16
F32 = jnp.float32
MESH = pl.DeviceIdType.MESH


def split3(x):
    hi = x.astype(BF).astype(F32)
    rest = x - hi
    mid = rest.astype(BF).astype(F32)
    return hi, mid, rest - mid


def dot(a, b):
    return jnp.dot(a, b, preferred_element_type=F32)


def kernel(
    zs, pipes,
    q_hbm, o_hbm, g_hbm, ln_ref, ok_hbm, ov_hbm, pk_hbm, pv_hbm, tab_ref, len_ref,
    dq_out, dok_out, dov_out, dpk_out, dpv_out,
    qb, ob, cb, qh, ch, qt, ct, kv, kaug, okv, dqt, ds_s, p_s, part,
    send_buf, recv_buf, y_buf, y_got, z_buf, z_got, fsend, frecv, fsum, fgot, dq_st, ok_st, ln_t, ln_r, bp_s, bp,
    loc_sem, sib_send, sib_recv, cot_send, cot_recv, kv_send, kv_recv,
    ga_send, ga_recv, rs_send, rs_recv, y_send, y_recv, z_send, z_recv, f_send, f_recv, out_sem, out_send, out_recv,
):
    p = lax.axis_index("pipe")
    c = lax.axis_index("ctx")
    core = lax.rem(c, 2)
    z = lax.rem(lax.div(c, 2), zs)
    yl = lax.div(c, 2 * zs)
    oc = 1 - core
    hops = zs // 2

    def dev(pp, yy, zz, kk):
        return (pp, (yy * zs + zz) * 2 + kk)

    sib = dev(p, yl, z, oc)
    z_up = lax.rem(z + 1, zs)
    z_dn = lax.rem(z + zs - 1, zs)
    p_up = lax.rem(p + 1, pipes)
    p_dn = lax.rem(p + pipes - 1, pipes)
    ring_dst = (dev(p, yl, z_up, core), dev(p, yl, z_dn, core))

    def lanes_at(ref, start, width):
        return ref.at[:, pl.ds(pl.multiple_of(start, 128), width)]

    def remote(src, dst, ss, rs, to):
        return pltpu.make_async_remote_copy(
            src_ref=src, dst_ref=dst, send_sem=ss, recv_sem=rs, device_id=to, device_id_type=MESH
        )

    my_rows = pl.ds(pl.multiple_of(core * ROWS, ROWS), ROWS)
    my_keys = pl.ds(pl.multiple_of(yl * 128 + core * 64, 64), 64)

    barrier = pltpu.get_barrier_semaphore()
    partners = [
        sib,
        dev(p, 1 - yl, z, 0), dev(p, 1 - yl, z, 1),
        ring_dst[0], ring_dst[1],
        dev(p_dn, yl, z, 0), dev(p_dn, yl, z, 1),
        dev(p_up, yl, z, 0), dev(p_up, yl, z, 1),
    ]
    for to in partners:
        pl.semaphore_signal(barrier, inc=1, device_id=to, device_id_type=MESH)

    loc = [
        pltpu.make_async_copy(lanes_at(q_hbm, core * 2048, 2048), qb.at[my_rows], loc_sem.at[0]),
        pltpu.make_async_copy(lanes_at(o_hbm, core * 2048, 2048), ob.at[my_rows], loc_sem.at[1]),
        pltpu.make_async_copy(lanes_at(ok_hbm, core * 256, 256), okv.at[my_rows, 0:256], loc_sem.at[2]),
        pltpu.make_async_copy(lanes_at(ov_hbm, core * 256, 256), okv.at[my_rows, 256:512], loc_sem.at[3]),
    ]
    kv_loc = [
        [
            pltpu.make_async_copy(
                lanes_at(src, core * 256 + h * 128, 128),
                kv.at[h, z, my_keys, j * 128 : (j + 1) * 128],
                loc_sem.at[4 + 2 * h + j],
            )
            for j, src in enumerate((pk_hbm, pv_hbm))
        ]
        for h in range(2)
    ]
    for cp in kv_loc[0] + kv_loc[1] + loc:
        cp.start()

    row = lax.broadcasted_iota(jnp.int32, (32, ROWS), 1)
    length = jnp.where(row < RLEN, len_ref[0, 0], len_ref[0, 1])
    live = lax.rem(row, RLEN) < length
    ln_t[...] = jnp.where(live, ln_ref[...] * (1.0 / SCALE), FAR)
    lane = lax.broadcasted_iota(jnp.int32, bp_s.shape, 1)
    ids = lax.broadcasted_iota(jnp.int32, (bp_s.shape[0], tab_ref.shape[1]), 0)
    offs = jnp.zeros(bp_s.shape, F32)
    for rr in range(2):
        hit = jnp.where(tab_ref[rr : rr + 1, :] == ids, 1.0, 0.0)
        listed = jnp.max(hit, axis=1, keepdims=True)
        offs = jnp.where(lane == 3 + 2 * core + rr, (listed - 1.0) * FAR, offs)
    bp_s[...] = offs
    bp[core] = offs
    ln_r[core] = ln_t[pl.ds(pl.multiple_of(core * 16, 16), 16), :]

    pl.semaphore_wait(barrier, len(partners))

    group = [(yl, oc), (1 - yl, core), (1 - yl, oc)]
    kv_out = [
        [
            remote(
                lanes_at(src, kk * 256 + h * 128, 128),
                kv.at[h, z, my_keys, j * 128 : (j + 1) * 128],
                kv_send.at[i, h, j], kv_recv.at[i, h, j], dev(p, yy, z, kk),
            )
            for i, (yy, kk) in enumerate(group)
            for j, src in enumerate((pk_hbm, pv_hbm))
        ]
        for h in range(2)
    ]
    for cp in kv_out[0] + kv_out[1]:
        cp.start()

    sib_out = [
        remote(lanes_at(q_hbm, oc * 2048, 2048), qb.at[my_rows], sib_send.at[0], sib_recv.at[0], sib),
        remote(lanes_at(o_hbm, oc * 2048, 2048), ob.at[my_rows], sib_send.at[1], sib_recv.at[1], sib),
        remote(lanes_at(ok_hbm, oc * 256, 256), okv.at[my_rows, 0:256], sib_send.at[2], sib_recv.at[2], sib),
        remote(lanes_at(ov_hbm, oc * 256, 256), okv.at[my_rows, 256:512], sib_send.at[3], sib_recv.at[3], sib),
        remote(ln_t.at[pl.ds(pl.multiple_of(oc * 16, 16), 16)], ln_r.at[core], sib_send.at[4], sib_recv.at[4], sib),
        remote(bp_s, bp.at[core], sib_send.at[5], sib_recv.at[5], sib),
    ]
    for i in (4, 5, 0, 2, 3, 1):
        sib_out[i].start()

    cot_out = [
        [
            remote(
                lanes_at(g_hbm, kk * 2048 + part_i * 512, 512),
                cb.at[my_rows, part_i * 512 : (part_i + 1) * 512],
                cot_send.at[part_i, d], cot_recv.at[part_i, d], dev(p_dn, yl, z, kk),
            )
            for d, kk in enumerate((oc, core))
        ]
        for part_i in range(4)
    ]

    def cot_wait(i):
        for cp in cot_out[i]:
            cp.wait_recv()

    def gather(h, d, t):
        chunk = lax.rem(z + zs - (t - 1), zs) if d == 0 else lax.rem(z + t - 1, zs)
        rows = slice(0, 256) if t < hops else slice(d * 128, (d + 1) * 128)
        ref = kv.at[h, chunk, rows]
        return remote(ref, ref, ga_send.at[h, d, t - 1], ga_recv.at[h, d, t - 1], ring_dst[d])

    def gather_wait(h, d, t):
        chunk = lax.rem(z + zs - t, zs) if d == 0 else lax.rem(z + t, zs)
        rows = slice(0, 256) if t < hops else slice(d * 128, (d + 1) * 128)
        ref = kv.at[h, chunk, rows]
        remote(ref, ref, ga_send.at[h, d, t - 1], ga_recv.at[h, d, t - 1], ring_dst[d]).wait_recv()

    def gather_pass(h, t):
        for d in range(2):
            gather_wait(h, d, t)
            if t < hops:
                gather(h, d, t + 1).start()

    for h in range(2):
        for cp in kv_loc[h]:
            cp.wait()
        for cp in kv_out[h]:
            cp.wait_recv()
        for d in range(2):
            gather(h, d, 1).start()
    for i in range(4):
        for cp in cot_out[i]:
            cp.start()

    qt[:, 128:256, :] = jnp.zeros((2, 128, 2048), BF)
    ct[:, 128:256, :] = jnp.zeros((2, 128, 2048), BF)
    dqt[...] = jnp.zeros(dqt.shape, F32)
    sub = lax.broadcasted_iota(jnp.int32, (16, 128), 0)
    col = lax.broadcasted_iota(jnp.int32, (16, 128), 1)

    def tile_cols(side, g):
        start = (g // 4) * 1024 + side * 512 + (g % 4) * 128
        return slice(start, start + 128)

    def query_tiles(h, side):
        for g in range(GROUP):
            cols = tile_cols(side, g)
            tile = qb[side * 128 : (side + 1) * 128, (h * 8 + g) * 128 : (h * 8 + g + 1) * 128]
            qh[h, cols, :] = tile
            qt[h, 0:128, cols] = tile.T
            hi, mid, low = split3(ln_r[side, h * 8 + g : h * 8 + g + 1, :])
            own = jnp.where(sub - 3 == side * 2 + lax.div(col, RLEN), 1.0, 0.0)
            aug = jnp.where(sub == 0, -hi, jnp.where(sub == 1, -mid, jnp.where(sub == 2, -low, own)))
            qt[h, 128:144, cols] = aug.astype(BF)

    def cot_tiles(h, q):
        for side, g in [(side, g) for side in range(2) for g in range(q * 4, q * 4 + 4)]:
            cols = tile_cols(side, g)
            rows, lanes = slice(side * 128, (side + 1) * 128), slice((h * 8 + g) * 128, (h * 8 + g + 1) * 128)
            tile = cb[rows, lanes]
            ch[h, cols, :] = tile
            tile_t = tile.T
            ct[h, 0:128, cols] = tile_t
            prod = tile_t.astype(F32) * ob[rows, lanes].T.astype(F32)
            hi, mid, low = split3(jnp.sum(prod, axis=0, keepdims=True))
            aug = jnp.where(sub == 0, hi, jnp.where(sub == 1, mid, jnp.where(sub == 2, low, 0.0)))
            ct[h, 128:144, cols] = aug.astype(BF)

    sib_out[4].wait_recv()
    sib_out[5].wait_recv()
    aug_lane = lax.broadcasted_iota(jnp.int32, bp_s.shape, 1)
    blocks = bp[0] + bp[1] + jnp.where(aug_lane < 3, 1.0, 0.0)
    spread = jnp.broadcast_to(blocks[:, None, :], (blocks.shape[0], BLK, 128))
    spread = spread.reshape(2, zs, 128, 128).astype(BF)
    for yy in range(2):
        kaug[:, yy * 128 : (yy + 1) * 128, :] = spread[yy]

    loc[0].wait()
    sib_out[0].wait_recv()
    for side in range(2):
        query_tiles(0, side)
    if hops > 2:
        gather_pass(0, 1)
    for side in range(2):
        query_tiles(1, side)
    if hops > 2:
        gather_pass(1, 1)

    loc[1].wait()
    for i in (1, 2, 3):
        sib_out[i].wait_recv()
    loc[2].wait()
    loc[3].wait()

    one_lane = lax.broadcasted_iota(jnp.int32, (256, 128), 1) < 3
    v_cst = jnp.where(one_lane, -1.0, 0.0).astype(BF)
    k_cst = jnp.where(one_lane, 1.0, 0.0).astype(BF)

    def own_part(h):
        key_i = lax.broadcasted_iota(jnp.int32, (ROWS, 512), 0)
        row_i = lax.rem(lax.broadcasted_iota(jnp.int32, (ROWS, 512), 1), ROWS)
        seen = (lax.div(key_i, RLEN) == lax.div(row_i, RLEN)) & (key_i <= row_i)
        for side in range(2):
            rows = slice(side * 128, (side + 1) * 128)
            k_l = okv[rows, h * 128 : (h + 1) * 128]
            v_l = okv[rows, 256 + h * 128 : 256 + (h + 1) * 128]
            k_full = jnp.concatenate([k_l, k_cst[:128]], 1)
            v_full = jnp.concatenate([v_l, v_cst[:128]], 1)
            dk = jnp.zeros((ROWS, HD), F32)
            dv = jnp.zeros((ROWS, HD), F32)
            for q in range(2):
                cols = slice(q * 1024 + side * 512, q * 1024 + (side + 1) * 512)
                pr = jnp.where(seen, jnp.exp2(dot(k_full, qt[h, :, cols]) * EXP_SCALE), 0.0)
                ds = (pr * dot(v_full, ct[h, :, cols])).astype(BF)
                dqt[h, :, cols] += dot(k_l.T, ds)
                dk += dot(ds, qh[h, cols, :])
                dv += dot(pr.astype(BF), ch[h, cols, :])
            ok_st[side, :, h * 128 : (h + 1) * 128] = (dk * SCALE).astype(BF)
            ok_st[side, :, 256 + h * 128 : 256 + (h + 1) * 128] = dv.astype(BF)

    def unit(h, k, q=None):
        lo, hi = (0, 2048) if q is None else (q * 1024, (q + 1) * 1024)
        above = lax.rem(2 * k, zs)
        places = (2 * k - 1, above)
        ids = (lax.rem(z + zs - k, zs), lax.rem(z + lax.div(above, 2), zs))
        k_l = jnp.concatenate([kv[h, i, :, 0:128] for i in ids], 0)
        v_l = jnp.concatenate([kv[h, i, :, 128:256] for i in ids], 0)
        k_full = jnp.concatenate([k_l, jnp.concatenate([kaug[i] for i in ids], 0)], 1)
        v_full = jnp.concatenate([v_l, jnp.concatenate([v_cst, v_cst], 0)], 1)
        for n in range(lo, hi, 512):
            cols = slice(n, n + 512)
            pr = jnp.exp2(dot(k_full, qt[h, :, cols]) * EXP_SCALE)
            dp = dot(v_full, ct[h, :, cols])
            p_s[:, cols] = pr.astype(BF)
            ds_s[:, cols] = (pr * dp).astype(BF)
        dqt[h, :, lo:hi] += dot(k_l.T, ds_s[:, lo:hi])
        dk = dot(ds_s[:, lo:hi], qh[h, lo:hi])
        dv = dot(p_s[:, lo:hi], ch[h, lo:hi])
        for i, j in enumerate(places):
            keys = slice(i * 256, (i + 1) * 256)
            if q == 1:
                part[h, j, :, 0:128] += dk[keys]
                part[h, j, :, 128:256] += dv[keys]
            else:
                part[h, j, :, 0:128] = dk[keys]
                part[h, j, :, 128:256] = dv[keys]

    def rs_rows(d, k):
        return slice(0, 256) if k < hops else slice(d * 128, (d + 1) * 128)

    def place(d, k):
        return zs - 1 if k == hops else (2 * k if d == 0 else 2 * k - 1)

    def rs_copy(d, k):
        rows = rs_rows(d, k)
        return remote(
            send_buf.at[d, k - 1, rows], recv_buf.at[d, k - 1, rows],
            rs_send.at[d, k - 1], rs_recv.at[d, k - 1], ring_dst[d],
        )

    def rs_stage(d, k):
        j = place(d, k)
        rows = rs_rows(d, k)
        send_buf[d, k - 1, rows] = part[0, j, rows].astype(BF)
        if k < hops:
            rs_copy(d, k + 1).wait_recv()
            got = rs_rows(d, k + 1)
            total = part[0, j, got] + recv_buf[d, k, got].astype(F32)
            send_buf[d, k - 1, got] = total.astype(BF)
        rs_copy(d, k).start()

    me4 = yl * 2 + core
    f_out = [
        remote(
            fsend.at[pl.ds(pl.multiple_of(yy * 128 + kk * 64, 64), 64)],
            frecv.at[me4], f_send.at[i], f_recv.at[i], dev(p, yy, z, kk),
        )
        for i, (yy, kk) in enumerate(group)
    ]

    def rs_last():
        for d in range(2):
            rs_copy(d, 1).wait_recv()
            got = rs_rows(d, 1)
            part[0, 0, got] += recv_buf[d, 0, got].astype(F32)
        fsend[...] = part[0, 0].astype(BF)
        for cp in f_out:
            cp.start()
        frecv[me4] = fsend[my_keys, :]

    def pool_out(h, kk, tot):
        lanes = slice((2 * kk + h) * 128, (2 * kk + h + 1) * 128)
        dpk_out[:, lanes] = tot[:, 0:128] * SCALE
        dpv_out[:, lanes] = tot[:, 128:256]

    def rs_finish():
        for cp in f_out:
            cp.wait_recv()
        for kk in range(2):
            pool_out(0, kk, frecv[kk].astype(F32) + frecv[2 + kk].astype(F32))

    def y_copy(j):
        return remote(y_buf.at[j], y_got.at[j], y_send.at[j], y_recv.at[j], dev(p, 1 - yl, z, core))

    def own_rows(rows):
        return pl.ds(pl.multiple_of(yl * 128 + rows.start, 64), rows.stop - rows.start)

    def y_start(j):
        other = pl.ds(pl.multiple_of((1 - yl) * 128, 128), 128)
        y_buf[j] = part[1, j, other].astype(BF)
        y_copy(j).start()

    def y_add(j):
        y_copy(j).wait_recv()
        mine = own_rows(slice(0, 128))
        part[1, j, mine] = part[1, j, mine] + y_got[j].astype(F32)

    def z_rows(d, k):
        return slice(0, 128) if k < hops else slice(d * 64, (d + 1) * 64)

    def z_copy(d, k):
        rows = z_rows(d, k)
        return remote(
            z_buf.at[d, k - 1, rows], z_got.at[d, k - 1, rows],
            z_send.at[d, k - 1], z_recv.at[d, k - 1], ring_dst[d],
        )

    def z_stage(d, k):
        j = place(d, k)
        rows = z_rows(d, k)
        if k < hops or d == 0:
            y_add(j)
        z_buf[d, k - 1, rows] = part[1, j, own_rows(rows)].astype(BF)
        if k < hops:
            z_copy(d, k + 1).wait_recv()
            got = z_rows(d, k + 1)
            total = part[1, j, own_rows(got)] + z_got[d, k, got].astype(F32)
            z_buf[d, k - 1, got] = total.astype(BF)
        z_copy(d, k).start()

    sum_out = remote(
        fsum.at[pl.ds(pl.multiple_of(oc * 64, 64), 64)], fgot.at[core], f_send.at[3], f_recv.at[3], sib
    )

    def z_last():
        y_add(0)
        fsum[...] = part[1, 0, own_rows(slice(0, 128))]
        for d in range(2):
            z_copy(d, 1).wait_recv()
            got = z_rows(d, 1)
            fsum[got] += z_got[d, 0, got].astype(F32)
        sum_out.start()
        fgot[core] = fsum[pl.ds(pl.multiple_of(core * 64, 64), 64), :]

    def z_finish():
        sum_out.wait_recv()
        for kk in range(2):
            pool_out(1, kk, fgot[kk])

    def dq_tiles(h):
        for side in range(2):
            for g in range(GROUP):
                tile = dqt[h, :, tile_cols(side, g)] * SCALE
                dq_st[side, :, (h * 8 + g) * 128 : (h * 8 + g + 1) * 128] = tile.T.astype(BF)

    def dq_copies(h):
        lanes = slice(h * 1024, (h + 1) * 1024)
        dst = lanes_at(dq_out, core * 2048 + h * 1024, 1024)
        return [
            remote(dq_st.at[oc, :, lanes], dst, out_send.at[2 + h], out_recv.at[2 + h], sib),
            pltpu.make_async_copy(dq_st.at[core, :, lanes], dst, out_sem.at[2 + h]),
        ]

    near = hops - 2
    cot_wait(0)
    cot_tiles(0, 0)

    def near_first(i, carry):
        if near > 1:
            @pl.when(i == 1)
            def _():
                gather_pass(0, 2)

        unit(0, i + 1, 0)
        return carry

    def near_second(i, carry):
        unit(0, i + 1, 1)
        return carry

    def far(i, carry):
        @pl.when(i == 1)
        def _():
            gather_pass(1, hops - 1)
            gather_pass(0, hops)

        unit(0, hops - 1 + i)
        return carry

    if near > 0:
        lax.fori_loop(0, near, near_first, 0)
    if near > 1:
        gather_pass(1, 2)
    cot_wait(1)
    cot_tiles(0, 1)
    if near > 0:
        lax.fori_loop(0, near, near_second, 0)
    own_part(0)
    gather_pass(0, hops - 1)
    lax.fori_loop(0, 2, far, 0)
    for d in range(2):
        rs_stage(d, hops)

    gather_pass(1, hops)
    cot_wait(2)
    cot_tiles(1, 0)

    def far_first(i, carry):
        unit(1, hops - i, 0)

        @pl.when(i == 0)
        def _():
            for d in range(2):
                rs_stage(d, hops - 1)

        return carry

    def far_second(i, carry):
        unit(1, hops - i, 1)
        y_start(2 * (hops - i) - 1)

        @pl.when(i == 1)
        def _():
            y_start(2 * (hops - 1))
            if hops > 2:
                for d in range(2):
                    rs_stage(d, hops - 2)

        return carry

    def near_both(i, carry):
        k = near - i
        unit(1, k)
        y_start(2 * k - 1)
        y_start(2 * k)
        for n in range(2):
            @pl.when(i == n)
            def _(n=n):
                for d in range(2):
                    z_stage(d, hops - n)
                if n == 1:
                    for d in range(2):
                        rs_stage(d, hops - 3)

        return carry

    lax.fori_loop(0, 2, far_first, 0)
    cot_wait(3)
    cot_tiles(1, 1)
    lax.fori_loop(0, 2, far_second, 0)
    if near > 0:
        lax.fori_loop(0, near, near_both, 0)
    y_start(0)

    own_part(1)
    ok_out = []
    for j, out in enumerate((dok_out, dov_out)):
        lanes = slice(j * 256, (j + 1) * 256)
        dst = lanes_at(out, core * 256, 256)
        ok_out.append(remote(ok_st.at[oc, :, lanes], dst, out_send.at[j], out_recv.at[j], sib))
        ok_out.append(pltpu.make_async_copy(ok_st.at[core, :, lanes], dst, out_sem.at[j]))
    for cp in ok_out:
        cp.start()
    for k in (2, 1):
        dq_tiles(2 - k)
        for cp in dq_copies(2 - k):
            cp.start()
        for d in range(2):
            z_stage(d, k)
        if k == 2:
            rs_last()
    rs_finish()
    z_last()
    for cp in ok_out + dq_copies(0) + dq_copies(1):
        cp.wait()
    for cp in kv_out[0] + kv_out[1] + sum(cot_out, []) + sib_out + f_out:
        cp.wait_send()
    for d in range(2):
        for t in range(1, hops + 1):
            for h in range(2):
                gather(h, d, t).wait_send()
            rs_copy(d, t).wait_send()
            z_copy(d, t).wait_send()
    for j in range(zs):
        y_copy(j).wait_send()
    z_finish()
    sum_out.wait_send()


def hand_over(*refs):
    for src, dst in zip(refs[:5], refs[5:]):
        dst[...] = src[...]


def local(zs, pipes, q, o, g, ln, ok, ov, pk, pv, tab, lens):
    any_ = pl.BlockSpec(memory_space=pl.ANY)
    vmem = pl.BlockSpec(memory_space=pltpu.VMEM)
    smem = pl.BlockSpec(memory_space=pltpu.SMEM)
    hops = zs // 2
    blocks = zs * 256 // BLK
    dma = pltpu.SemaphoreType.DMA
    outs = pl.pallas_call(
        functools.partial(kernel, zs, pipes),
        out_shape=(
            jax.ShapeDtypeStruct((ROWS, 4096), BF),
            jax.ShapeDtypeStruct((ROWS, 512), BF),
            jax.ShapeDtypeStruct((ROWS, 512), BF),
            jax.ShapeDtypeStruct((64, 512), F32),
            jax.ShapeDtypeStruct((64, 512), F32),
        ),
        in_specs=[any_, any_, any_, vmem, any_, any_, any_, any_, vmem, smem],
        out_specs=(any_, any_, any_, vmem, vmem),
        scratch_shapes=[
            pltpu.VMEM((256, 2048), BF),
            pltpu.VMEM((256, 2048), BF),
            pltpu.VMEM((256, 2048), BF),
            pltpu.VMEM((2, 2048, 128), BF),
            pltpu.VMEM((2, 2048, 128), BF),
            pltpu.VMEM((2, 256, 2048), BF),
            pltpu.VMEM((2, 256, 2048), BF),
            pltpu.VMEM((2, zs, 256, 256), BF),
            pltpu.VMEM((zs, 256, 128), BF),
            pltpu.VMEM((256, 512), BF),
            pltpu.VMEM((2, 128, 2048), F32),
            pltpu.VMEM((512, 2048), BF),
            pltpu.VMEM((512, 2048), BF),
            pltpu.VMEM((2, zs, 256, 256), F32),
            pltpu.VMEM((2, hops, 256, 256), BF),
            pltpu.VMEM((2, hops, 256, 256), BF),
            pltpu.VMEM((zs, 128, 256), BF),
            pltpu.VMEM((zs, 128, 256), BF),
            pltpu.VMEM((2, hops, 128, 256), BF),
            pltpu.VMEM((2, hops, 128, 256), BF),
            pltpu.VMEM((256, 256), BF),
            pltpu.VMEM((4, 64, 256), BF),
            pltpu.VMEM((128, 256), F32),
            pltpu.VMEM((2, 64, 256), F32),
            pltpu.VMEM((2, 128, 2048), BF),
            pltpu.VMEM((2, 128, 512), BF),
            pltpu.VMEM((32, 128), F32),
            pltpu.VMEM((2, 16, 128), F32),
            pltpu.VMEM((blocks, 128), F32),
            pltpu.VMEM((2, blocks, 128), F32),
            dma((8,)), dma((6,)), dma((6,)), dma((4, 2)), dma((4, 2)), dma((3, 2, 2)), dma((3, 2, 2)),
            dma((2, 2, hops)), dma((2, 2, hops)), dma((2, hops)), dma((2, hops)),
            dma((zs,)), dma((zs,)), dma((2, hops)), dma((2, hops)),
            dma((4,)), dma((4,)), dma((4,)), dma((4,)), dma((4,)),
        ],
        compiler_params=pltpu.CompilerParams(
            collective_id=0, has_side_effects=True, vmem_limit_bytes=56 * 1024 * 1024
        ),
    )(q[0], o[0], g[0], ln[0].T, ok[0], ov[0], pk[0], pv[0], tab[0], lens)
    halves = [pl.BlockSpec((out.shape[0] // 2, out.shape[1]), lambda i: (i, 0)) for out in outs]
    outs = pl.pallas_call(
        hand_over,
        out_shape=tuple(jax.ShapeDtypeStruct(out.shape, out.dtype) for out in outs),
        grid=(2,),
        in_specs=halves,
        out_specs=tuple(halves),
    )(*outs)
    return tuple(out[None] for out in outs)


def solution(mesh):
    rows = P("pipe", "ctx", None)
    in_specs = (rows,) * 9 + (P("pipe", "ctx"),)
    fn = functools.partial(local, mesh.shape["ctx"] // 4, mesh.shape["pipe"])
    return jax.shard_map(fn, mesh=mesh, in_specs=in_specs, out_specs=(rows,) * 5, check_vma=False)
```

```python
import functools
import math

import jax
import jax.numpy as jnp
from jax import lax
from jax.experimental import pallas as pl
from jax.experimental.pallas import tpu as pltpu
from jax.sharding import PartitionSpec as P

HD = 128
ROWS = 128
RLEN = 64
BLK = 32
GROUP = 8
SCALE = HD ** -0.5
EXP_SCALE = SCALE * math.log2(math.e)
FAR = 1e30
BF = jnp.bfloat16
F32 = jnp.float32
MESH = pl.DeviceIdType.MESH


def split3(x):
    hi = x.astype(BF).astype(F32)
    rest = x - hi
    mid = rest.astype(BF).astype(F32)
    return hi, mid, rest - mid


def dot(a, b):
    return jnp.dot(a, b, preferred_element_type=F32)


def kernel(
    zs, pipes,
    q_hbm, o_hbm, g_hbm, ln_ref, ok_hbm, ov_hbm, pk_hbm, pv_hbm, tab_ref, len_ref,
    dq_out, dok_out, dov_out, dpk_out, dpv_out,
    qb, ob, cb, qh, ch, qt, ct, kv, kaug, okv, dqt, ds_s, p_s, part,
    send_buf, recv_buf, y_buf, y_got, z_buf, z_got, fsend, frecv, fsum, fgot, dq_st, ok_st, ln_t, ln_r, bp_s, bp,
    loc_sem, sib_send, sib_recv, cot_send, cot_recv, kv_send, kv_recv,
    ga_send, ga_recv, rs_send, rs_recv, y_send, y_recv, z_send, z_recv, f_send, f_recv, out_sem, out_send, out_recv,
):
    p = lax.axis_index("pipe")
    c = lax.axis_index("ctx")
    core = lax.rem(c, 2)
    z = lax.rem(lax.div(c, 2), zs)
    yl = lax.div(c, 2 * zs)
    oc = 1 - core
    hops = zs // 2

    def dev(pp, yy, zz, kk):
        return (pp, (yy * zs + zz) * 2 + kk)

    sib = dev(p, yl, z, oc)
    z_up = lax.rem(z + 1, zs)
    z_dn = lax.rem(z + zs - 1, zs)
    p_up = lax.rem(p + 1, pipes)
    p_dn = lax.rem(p + pipes - 1, pipes)
    ring_dst = (dev(p, yl, z_up, core), dev(p, yl, z_dn, core))

    def lanes_at(ref, start, width):
        return ref.at[:, pl.ds(pl.multiple_of(start, 128), width)]

    def remote(src, dst, ss, rs, to):
        return pltpu.make_async_remote_copy(
            src_ref=src, dst_ref=dst, send_sem=ss, recv_sem=rs, device_id=to, device_id_type=MESH
        )

    my_rows = pl.ds(pl.multiple_of(core * ROWS, ROWS), ROWS)
    my_keys = pl.ds(pl.multiple_of(yl * 128 + core * 64, 64), 64)

    barrier = pltpu.get_barrier_semaphore()
    partners = [
        sib,
        dev(p, 1 - yl, z, 0), dev(p, 1 - yl, z, 1),
        ring_dst[0], ring_dst[1],
        dev(p_dn, yl, z, 0), dev(p_dn, yl, z, 1),
        dev(p_up, yl, z, 0), dev(p_up, yl, z, 1),
    ]
    for to in partners:
        pl.semaphore_signal(barrier, inc=1, device_id=to, device_id_type=MESH)

    loc = [
        pltpu.make_async_copy(lanes_at(q_hbm, core * 2048, 2048), qb.at[my_rows], loc_sem.at[0]),
        pltpu.make_async_copy(lanes_at(o_hbm, core * 2048, 2048), ob.at[my_rows], loc_sem.at[1]),
        pltpu.make_async_copy(lanes_at(ok_hbm, core * 256, 256), okv.at[my_rows, 0:256], loc_sem.at[2]),
        pltpu.make_async_copy(lanes_at(ov_hbm, core * 256, 256), okv.at[my_rows, 256:512], loc_sem.at[3]),
    ]
    kv_loc = [
        [
            pltpu.make_async_copy(
                lanes_at(src, core * 256 + h * 128, 128),
                kv.at[h, z, my_keys, j * 128 : (j + 1) * 128],
                loc_sem.at[4 + 2 * h + j],
            )
            for j, src in enumerate((pk_hbm, pv_hbm))
        ]
        for h in range(2)
    ]
    for cp in kv_loc[0] + kv_loc[1] + loc:
        cp.start()

    row = lax.broadcasted_iota(jnp.int32, (32, ROWS), 1)
    length = jnp.where(row < RLEN, len_ref[0, 0], len_ref[0, 1])
    live = lax.rem(row, RLEN) < length
    ln_t[...] = jnp.where(live, ln_ref[...] * (1.0 / SCALE), FAR)
    lane = lax.broadcasted_iota(jnp.int32, bp_s.shape, 1)
    ids = lax.broadcasted_iota(jnp.int32, (bp_s.shape[0], tab_ref.shape[1]), 0)
    offs = jnp.zeros(bp_s.shape, F32)
    for rr in range(2):
        hit = jnp.where(tab_ref[rr : rr + 1, :] == ids, 1.0, 0.0)
        listed = jnp.max(hit, axis=1, keepdims=True)
        offs = jnp.where(lane == 3 + 2 * core + rr, (listed - 1.0) * FAR, offs)
    bp_s[...] = offs
    bp[core] = offs
    ln_r[core] = ln_t[pl.ds(pl.multiple_of(core * 16, 16), 16), :]

    pl.semaphore_wait(barrier, len(partners))

    group = [(yl, oc), (1 - yl, core), (1 - yl, oc)]
    kv_out = [
        [
            remote(
                lanes_at(src, kk * 256 + h * 128, 128),
                kv.at[h, z, my_keys, j * 128 : (j + 1) * 128],
                kv_send.at[i, h, j], kv_recv.at[i, h, j], dev(p, yy, z, kk),
            )
            for i, (yy, kk) in enumerate(group)
            for j, src in enumerate((pk_hbm, pv_hbm))
        ]
        for h in range(2)
    ]
    for cp in kv_out[0] + kv_out[1]:
        cp.start()

    sib_out = [
        remote(lanes_at(q_hbm, oc * 2048, 2048), qb.at[my_rows], sib_send.at[0], sib_recv.at[0], sib),
        remote(lanes_at(o_hbm, oc * 2048, 2048), ob.at[my_rows], sib_send.at[1], sib_recv.at[1], sib),
        remote(lanes_at(ok_hbm, oc * 256, 256), okv.at[my_rows, 0:256], sib_send.at[2], sib_recv.at[2], sib),
        remote(lanes_at(ov_hbm, oc * 256, 256), okv.at[my_rows, 256:512], sib_send.at[3], sib_recv.at[3], sib),
        remote(ln_t.at[pl.ds(pl.multiple_of(oc * 16, 16), 16)], ln_r.at[core], sib_send.at[4], sib_recv.at[4], sib),
        remote(bp_s, bp.at[core], sib_send.at[5], sib_recv.at[5], sib),
    ]
    for i in (4, 5, 0, 2, 3, 1):
        sib_out[i].start()

    cot_out = [
        [
            remote(
                lanes_at(g_hbm, kk * 2048 + part_i * 512, 512),
                cb.at[my_rows, part_i * 512 : (part_i + 1) * 512],
                cot_send.at[part_i, d], cot_recv.at[part_i, d], dev(p_dn, yl, z, kk),
            )
            for d, kk in enumerate((oc, core))
        ]
        for part_i in range(4)
    ]

    def cot_wait(i):
        for cp in cot_out[i]:
            cp.wait_recv()

    def gather(h, d, t):
        chunk = lax.rem(z + zs - (t - 1), zs) if d == 0 else lax.rem(z + t - 1, zs)
        rows = slice(0, 256) if t < hops else slice(d * 128, (d + 1) * 128)
        ref = kv.at[h, chunk, rows]
        return remote(ref, ref, ga_send.at[h, d, t - 1], ga_recv.at[h, d, t - 1], ring_dst[d])

    def gather_wait(h, d, t):
        chunk = lax.rem(z + zs - t, zs) if d == 0 else lax.rem(z + t, zs)
        rows = slice(0, 256) if t < hops else slice(d * 128, (d + 1) * 128)
        ref = kv.at[h, chunk, rows]
        remote(ref, ref, ga_send.at[h, d, t - 1], ga_recv.at[h, d, t - 1], ring_dst[d]).wait_recv()

    def gather_pass(h, t):
        for d in range(2):
            gather_wait(h, d, t)
            if t < hops:
                gather(h, d, t + 1).start()

    for h in range(2):
        for cp in kv_loc[h]:
            cp.wait()
        for cp in kv_out[h]:
            cp.wait_recv()
        for d in range(2):
            gather(h, d, 1).start()
    for i in range(4):
        for cp in cot_out[i]:
            cp.start()

    qt[:, 128:256, :] = jnp.zeros((2, 128, 2048), BF)
    ct[:, 128:256, :] = jnp.zeros((2, 128, 2048), BF)
    dqt[...] = jnp.zeros(dqt.shape, F32)
    sub = lax.broadcasted_iota(jnp.int32, (16, 128), 0)
    col = lax.broadcasted_iota(jnp.int32, (16, 128), 1)

    def tile_cols(side, g):
        start = (g // 4) * 1024 + side * 512 + (g % 4) * 128
        return slice(start, start + 128)

    def query_tiles(h, side):
        for g in range(GROUP):
            cols = tile_cols(side, g)
            tile = qb[side * 128 : (side + 1) * 128, (h * 8 + g) * 128 : (h * 8 + g + 1) * 128]
            qh[h, cols, :] = tile
            qt[h, 0:128, cols] = tile.T
            hi, mid, low = split3(ln_r[side, h * 8 + g : h * 8 + g + 1, :])
            own = jnp.where(sub - 3 == side * 2 + lax.div(col, RLEN), 1.0, 0.0)
            aug = jnp.where(sub == 0, -hi, jnp.where(sub == 1, -mid, jnp.where(sub == 2, -low, own)))
            qt[h, 128:144, cols] = aug.astype(BF)

    def cot_tiles(h, q):
        for side, g in [(side, g) for side in range(2) for g in range(q * 4, q * 4 + 4)]:
            cols = tile_cols(side, g)
            rows, lanes = slice(side * 128, (side + 1) * 128), slice((h * 8 + g) * 128, (h * 8 + g + 1) * 128)
            tile = cb[rows, lanes]
            ch[h, cols, :] = tile
            tile_t = tile.T
            ct[h, 0:128, cols] = tile_t
            prod = tile_t.astype(F32) * ob[rows, lanes].T.astype(F32)
            hi, mid, low = split3(jnp.sum(prod, axis=0, keepdims=True))
            aug = jnp.where(sub == 0, hi, jnp.where(sub == 1, mid, jnp.where(sub == 2, low, 0.0)))
            ct[h, 128:144, cols] = aug.astype(BF)

    sib_out[4].wait_recv()
    sib_out[5].wait_recv()
    aug_lane = lax.broadcasted_iota(jnp.int32, bp_s.shape, 1)
    blocks = bp[0] + bp[1] + jnp.where(aug_lane < 3, 1.0, 0.0)
    spread = jnp.broadcast_to(blocks[:, None, :], (blocks.shape[0], BLK, 128))
    spread = spread.reshape(2, zs, 128, 128).astype(BF)
    for yy in range(2):
        kaug[:, yy * 128 : (yy + 1) * 128, :] = spread[yy]

    loc[0].wait()
    sib_out[0].wait_recv()
    for side in range(2):
        query_tiles(0, side)
    if hops > 2:
        gather_pass(0, 1)
    for side in range(2):
        query_tiles(1, side)
    if hops > 2:
        gather_pass(1, 1)

    loc[1].wait()
    for i in (1, 2, 3):
        sib_out[i].wait_recv()
    loc[2].wait()
    loc[3].wait()

    one_lane = lax.broadcasted_iota(jnp.int32, (256, 128), 1) < 3
    v_cst = jnp.where(one_lane, -1.0, 0.0).astype(BF)
    k_cst = jnp.where(one_lane, 1.0, 0.0).astype(BF)

    def own_part(h):
        key_i = lax.broadcasted_iota(jnp.int32, (ROWS, 512), 0)
        row_i = lax.rem(lax.broadcasted_iota(jnp.int32, (ROWS, 512), 1), ROWS)
        seen = (lax.div(key_i, RLEN) == lax.div(row_i, RLEN)) & (key_i <= row_i)
        for side in range(2):
            rows = slice(side * 128, (side + 1) * 128)
            k_l = okv[rows, h * 128 : (h + 1) * 128]
            v_l = okv[rows, 256 + h * 128 : 256 + (h + 1) * 128]
            k_full = jnp.concatenate([k_l, k_cst[:128]], 1)
            v_full = jnp.concatenate([v_l, v_cst[:128]], 1)
            dk = jnp.zeros((ROWS, HD), F32)
            dv = jnp.zeros((ROWS, HD), F32)
            for q in range(2):
                cols = slice(q * 1024 + side * 512, q * 1024 + (side + 1) * 512)
                pr = jnp.where(seen, jnp.exp2(dot(k_full, qt[h, :, cols]) * EXP_SCALE), 0.0)
                ds = (pr * dot(v_full, ct[h, :, cols])).astype(BF)
                dqt[h, :, cols] += dot(k_l.T, ds)
                dk += dot(ds, qh[h, cols, :])
                dv += dot(pr.astype(BF), ch[h, cols, :])
            ok_st[side, :, h * 128 : (h + 1) * 128] = (dk * SCALE).astype(BF)
            ok_st[side, :, 256 + h * 128 : 256 + (h + 1) * 128] = dv.astype(BF)

    def unit(h, k, q=None):
        lo, hi = (0, 2048) if q is None else (q * 1024, (q + 1) * 1024)
        above = lax.rem(2 * k, zs)
        places = (2 * k - 1, above)
        ids = (lax.rem(z + zs - k, zs), lax.rem(z + lax.div(above, 2), zs))
        k_l = jnp.concatenate([kv[h, i, :, 0:128] for i in ids], 0)
        v_l = jnp.concatenate([kv[h, i, :, 128:256] for i in ids], 0)
        k_full = jnp.concatenate([k_l, jnp.concatenate([kaug[i] for i in ids], 0)], 1)
        v_full = jnp.concatenate([v_l, jnp.concatenate([v_cst, v_cst], 0)], 1)
        for n in range(lo, hi, 512):
            cols = slice(n, n + 512)
            pr = jnp.exp2(dot(k_full, qt[h, :, cols]) * EXP_SCALE)
            dp = dot(v_full, ct[h, :, cols])
            p_s[:, cols] = pr.astype(BF)
            ds_s[:, cols] = (pr * dp).astype(BF)
        dqt[h, :, lo:hi] += dot(k_l.T, ds_s[:, lo:hi])
        dk = dot(ds_s[:, lo:hi], qh[h, lo:hi])
        dv = dot(p_s[:, lo:hi], ch[h, lo:hi])
        for i, j in enumerate(places):
            keys = slice(i * 256, (i + 1) * 256)
            if q == 1:
                part[h, j, :, 0:128] += dk[keys]
                part[h, j, :, 128:256] += dv[keys]
            else:
                part[h, j, :, 0:128] = dk[keys]
                part[h, j, :, 128:256] = dv[keys]

    def rs_rows(d, k):
        return slice(0, 256) if k < hops else slice(d * 128, (d + 1) * 128)

    def place(d, k):
        return zs - 1 if k == hops else (2 * k if d == 0 else 2 * k - 1)

    def rs_copy(d, k):
        rows = rs_rows(d, k)
        return remote(
            send_buf.at[d, k - 1, rows], recv_buf.at[d, k - 1, rows],
            rs_send.at[d, k - 1], rs_recv.at[d, k - 1], ring_dst[d],
        )

    def rs_stage(d, k):
        j = place(d, k)
        rows = rs_rows(d, k)
        send_buf[d, k - 1, rows] = part[0, j, rows].astype(BF)
        if k < hops:
            rs_copy(d, k + 1).wait_recv()
            got = rs_rows(d, k + 1)
            total = part[0, j, got] + recv_buf[d, k, got].astype(F32)
            send_buf[d, k - 1, got] = total.astype(BF)
        rs_copy(d, k).start()

    me4 = yl * 2 + core
    f_out = [
        remote(
            fsend.at[pl.ds(pl.multiple_of(yy * 128 + kk * 64, 64), 64)],
            frecv.at[me4], f_send.at[i], f_recv.at[i], dev(p, yy, z, kk),
        )
        for i, (yy, kk) in enumerate(group)
    ]

    def rs_last():
        for d in range(2):
            rs_copy(d, 1).wait_recv()
            got = rs_rows(d, 1)
            part[0, 0, got] += recv_buf[d, 0, got].astype(F32)
        fsend[...] = part[0, 0].astype(BF)
        for cp in f_out:
            cp.start()
        frecv[me4] = fsend[my_keys, :]

    def pool_out(h, kk, tot):
        lanes = slice((2 * kk + h) * 128, (2 * kk + h + 1) * 128)
        dpk_out[:, lanes] = tot[:, 0:128] * SCALE
        dpv_out[:, lanes] = tot[:, 128:256]

    def rs_finish():
        for cp in f_out:
            cp.wait_recv()
        for kk in range(2):
            pool_out(0, kk, frecv[kk].astype(F32) + frecv[2 + kk].astype(F32))

    def y_copy(j):
        return remote(y_buf.at[j], y_got.at[j], y_send.at[j], y_recv.at[j], dev(p, 1 - yl, z, core))

    def own_rows(rows):
        return pl.ds(pl.multiple_of(yl * 128 + rows.start, 64), rows.stop - rows.start)

    def y_start(j):
        other = pl.ds(pl.multiple_of((1 - yl) * 128, 128), 128)
        y_buf[j] = part[1, j, other].astype(BF)
        y_copy(j).start()

    def y_add(j):
        y_copy(j).wait_recv()
        mine = own_rows(slice(0, 128))
        part[1, j, mine] = part[1, j, mine] + y_got[j].astype(F32)

    def z_rows(d, k):
        return slice(0, 128) if k < hops else slice(d * 64, (d + 1) * 64)

    def z_copy(d, k):
        rows = z_rows(d, k)
        return remote(
            z_buf.at[d, k - 1, rows], z_got.at[d, k - 1, rows],
            z_send.at[d, k - 1], z_recv.at[d, k - 1], ring_dst[d],
        )

    def z_stage(d, k):
        j = place(d, k)
        rows = z_rows(d, k)
        if k < hops or d == 0:
            y_add(j)
        z_buf[d, k - 1, rows] = part[1, j, own_rows(rows)].astype(BF)
        if k < hops:
            z_copy(d, k + 1).wait_recv()
            got = z_rows(d, k + 1)
            total = part[1, j, own_rows(got)] + z_got[d, k, got].astype(F32)
            z_buf[d, k - 1, got] = total.astype(BF)
        z_copy(d, k).start()

    sum_out = remote(
        fsum.at[pl.ds(pl.multiple_of(oc * 64, 64), 64)], fgot.at[core], f_send.at[3], f_recv.at[3], sib
    )

    def z_last():
        y_add(0)
        fsum[...] = part[1, 0, own_rows(slice(0, 128))]
        for d in range(2):
            z_copy(d, 1).wait_recv()
            got = z_rows(d, 1)
            fsum[got] += z_got[d, 0, got].astype(F32)
        sum_out.start()
        fgot[core] = fsum[pl.ds(pl.multiple_of(core * 64, 64), 64), :]

    def z_finish():
        sum_out.wait_recv()
        for kk in range(2):
            pool_out(1, kk, fgot[kk])

    def dq_tiles(h):
        for side in range(2):
            for g in range(GROUP):
                tile = dqt[h, :, tile_cols(side, g)] * SCALE
                dq_st[side, :, (h * 8 + g) * 128 : (h * 8 + g + 1) * 128] = tile.T.astype(BF)

    def dq_copies(h):
        lanes = slice(h * 1024, (h + 1) * 1024)
        dst = lanes_at(dq_out, core * 2048 + h * 1024, 1024)
        return [
            remote(dq_st.at[oc, :, lanes], dst, out_send.at[2 + h], out_recv.at[2 + h], sib),
            pltpu.make_async_copy(dq_st.at[core, :, lanes], dst, out_sem.at[2 + h]),
        ]

    near = hops - 2
    cot_wait(0)
    cot_tiles(0, 0)

    def near_first(i, carry):
        if near > 1:
            @pl.when(i == 1)
            def _():
                gather_pass(0, 2)

        unit(0, i + 1, 0)
        return carry

    def near_second(i, carry):
        unit(0, i + 1, 1)
        return carry

    def far(i, carry):
        @pl.when(i == 1)
        def _():
            gather_pass(1, hops - 1)
            gather_pass(0, hops)

        unit(0, hops - 1 + i)
        return carry

    if near > 0:
        lax.fori_loop(0, near, near_first, 0)
    if near > 1:
        gather_pass(1, 2)
    cot_wait(1)
    cot_tiles(0, 1)
    if near > 0:
        lax.fori_loop(0, near, near_second, 0)
    own_part(0)
    gather_pass(0, hops - 1)
    lax.fori_loop(0, 2, far, 0)
    for d in range(2):
        rs_stage(d, hops)

    gather_pass(1, hops)
    cot_wait(2)
    cot_tiles(1, 0)

    def far_first(i, carry):
        unit(1, hops - i, 0)

        @pl.when(i == 0)
        def _():
            for d in range(2):
                rs_stage(d, hops - 1)

        return carry

    def far_second(i, carry):
        unit(1, hops - i, 1)
        y_start(2 * (hops - i) - 1)

        @pl.when(i == 0)
        def _():
            if hops > 2:
                for d in range(2):
                    rs_stage(d, hops - 2)

        @pl.when(i == 1)
        def _():
            y_start(2 * (hops - 1))

        return carry

    def near_both(i, carry):
        k = near - i
        unit(1, k)
        y_start(2 * k - 1)
        y_start(2 * k)
        for n in range(near):
            @pl.when(i == n)
            def _(n=n):
                for d in range(2):
                    z_stage(d, hops - 1 - n)
                if n == 0 and hops > 3:
                    for d in range(2):
                        rs_stage(d, hops - 3)

        return carry

    lax.fori_loop(0, 2, far_first, 0)
    cot_wait(3)
    cot_tiles(1, 1)
    lax.fori_loop(0, 2, far_second, 0)
    for d in range(2):
        z_stage(d, hops)
    if near > 0:
        lax.fori_loop(0, near, near_both, 0)
    y_start(0)

    own_part(1)
    ok_out = []
    for j, out in enumerate((dok_out, dov_out)):
        lanes = slice(j * 256, (j + 1) * 256)
        dst = lanes_at(out, core * 256, 256)
        ok_out.append(remote(ok_st.at[oc, :, lanes], dst, out_send.at[j], out_recv.at[j], sib))
        ok_out.append(pltpu.make_async_copy(ok_st.at[core, :, lanes], dst, out_sem.at[j]))
    for cp in ok_out:
        cp.start()
    for h in range(2):
        dq_tiles(h)
        for cp in dq_copies(h):
            cp.start()
    for d in range(2):
        z_stage(d, 1)
    rs_last()
    rs_finish()
    z_last()
    for cp in ok_out + dq_copies(0) + dq_copies(1):
        cp.wait()
    for cp in kv_out[0] + kv_out[1] + sum(cot_out, []) + sib_out + f_out:
        cp.wait_send()
    for d in range(2):
        for t in range(1, hops + 1):
            for h in range(2):
                gather(h, d, t).wait_send()
            rs_copy(d, t).wait_send()
            z_copy(d, t).wait_send()
    for j in range(zs):
        y_copy(j).wait_send()
    z_finish()
    sum_out.wait_send()


def hand_over(*refs):
    for src, dst in zip(refs[:5], refs[5:]):
        dst[...] = src[...]


def local(zs, pipes, q, o, g, ln, ok, ov, pk, pv, tab, lens):
    any_ = pl.BlockSpec(memory_space=pl.ANY)
    vmem = pl.BlockSpec(memory_space=pltpu.VMEM)
    smem = pl.BlockSpec(memory_space=pltpu.SMEM)
    hops = zs // 2
    blocks = zs * 256 // BLK
    dma = pltpu.SemaphoreType.DMA
    outs = pl.pallas_call(
        functools.partial(kernel, zs, pipes),
        out_shape=(
            jax.ShapeDtypeStruct((ROWS, 4096), BF),
            jax.ShapeDtypeStruct((ROWS, 512), BF),
            jax.ShapeDtypeStruct((ROWS, 512), BF),
            jax.ShapeDtypeStruct((64, 512), F32),
            jax.ShapeDtypeStruct((64, 512), F32),
        ),
        in_specs=[any_, any_, any_, vmem, any_, any_, any_, any_, vmem, smem],
        out_specs=(any_, any_, any_, vmem, vmem),
        scratch_shapes=[
            pltpu.VMEM((256, 2048), BF),
            pltpu.VMEM((256, 2048), BF),
            pltpu.VMEM((256, 2048), BF),
            pltpu.VMEM((2, 2048, 128), BF),
            pltpu.VMEM((2, 2048, 128), BF),
            pltpu.VMEM((2, 256, 2048), BF),
            pltpu.VMEM((2, 256, 2048), BF),
            pltpu.VMEM((2, zs, 256, 256), BF),
            pltpu.VMEM((zs, 256, 128), BF),
            pltpu.VMEM((256, 512), BF),
            pltpu.VMEM((2, 128, 2048), F32),
            pltpu.VMEM((512, 2048), BF),
            pltpu.VMEM((512, 2048), BF),
            pltpu.VMEM((2, zs, 256, 256), F32),
            pltpu.VMEM((2, hops, 256, 256), BF),
            pltpu.VMEM((2, hops, 256, 256), BF),
            pltpu.VMEM((zs, 128, 256), BF),
            pltpu.VMEM((zs, 128, 256), BF),
            pltpu.VMEM((2, hops, 128, 256), BF),
            pltpu.VMEM((2, hops, 128, 256), BF),
            pltpu.VMEM((256, 256), BF),
            pltpu.VMEM((4, 64, 256), BF),
            pltpu.VMEM((128, 256), F32),
            pltpu.VMEM((2, 64, 256), F32),
            pltpu.VMEM((2, 128, 2048), BF),
            pltpu.VMEM((2, 128, 512), BF),
            pltpu.VMEM((32, 128), F32),
            pltpu.VMEM((2, 16, 128), F32),
            pltpu.VMEM((blocks, 128), F32),
            pltpu.VMEM((2, blocks, 128), F32),
            dma((8,)), dma((6,)), dma((6,)), dma((4, 2)), dma((4, 2)), dma((3, 2, 2)), dma((3, 2, 2)),
            dma((2, 2, hops)), dma((2, 2, hops)), dma((2, hops)), dma((2, hops)),
            dma((zs,)), dma((zs,)), dma((2, hops)), dma((2, hops)),
            dma((4,)), dma((4,)), dma((4,)), dma((4,)), dma((4,)),
        ],
        compiler_params=pltpu.CompilerParams(
            collective_id=0, has_side_effects=True, vmem_limit_bytes=56 * 1024 * 1024
        ),
    )(q[0], o[0], g[0], ln[0].T, ok[0], ov[0], pk[0], pv[0], tab[0], lens)
    halves = [pl.BlockSpec((out.shape[0] // 2, out.shape[1]), lambda i: (i, 0)) for out in outs]
    outs = pl.pallas_call(
        hand_over,
        out_shape=tuple(jax.ShapeDtypeStruct(out.shape, out.dtype) for out in outs),
        grid=(2,),
        in_specs=halves,
        out_specs=tuple(halves),
    )(*outs)
    return tuple(out[None] for out in outs)


def solution(mesh):
    rows = P("pipe", "ctx", None)
    in_specs = (rows,) * 9 + (P("pipe", "ctx"),)
    fn = functools.partial(local, mesh.shape["ctx"] // 4, mesh.shape["pipe"])
    return jax.shard_map(fn, mesh=mesh, in_specs=in_specs, out_specs=(rows,) * 5, check_vma=False)
```
